256 devices in a mesh: seq: 64 (over x, y_lo, z), ch: 4 (over y_hi, core).
Axes of the slice: x: 4, y: 4 (y_hi: 2, y_lo: 2; y = y_hi * 2 + y_lo), z: 8, core: 2. Of those that a mesh axis runs over, the one named last changes fastest.
Arguments:
- latents: bfloat16 [128, 1280, 16, 32], P('seq', 'ch'), may hold values from -16 to 16
- spatial_weight: bfloat16 [3, 3, 1280, 1280], P(None, None, 'ch'), may hold values from -0.078125 to 0.078125
- temporal_weight: bfloat16 [3, 1280, 1280], P(None, 'ch'), may hold values from -0.125 to 0.125
- mix_factor: float32 [1], replicated, may hold values from -1.5 to 1.5
Outputs:
- mixed_out: bfloat16 [128, 1280, 16, 32], P('seq', 'ch')
The draws below stay inside these ranges and needn't reach their ends.
All inputs are finite; a program needn't handle non-finite values.
Results may differ from the reference program's by a relative error of at most 0.012.
Values may be sent and summed in bfloat16 or wider, within the bound.
No kernel may reach another device: no remote copies, remote signals or barrier semaphores. Data moves between devices by JAX's collectives and lax.ppermute only.
A program may use at most 128 MiB of HBM per device.

```python
import math
import jax
import jax.numpy as jnp
from jax import lax

CH = 1280
GROUPS = 32
ROWS = 16
COLS = 32
FRAMES = 128


def draw_latents(key, part):
    key = jax.random.fold_in(key, 11)
    first, second, third = jax.random.split(key, 3)
    frame_pos = jnp.arange(FRAMES, dtype=jnp.float32) / max(FRAMES - 1, 1)
    chan_scale = jnp.exp(jax.random.uniform(second, (1, CH, 1, 1), jnp.float32, math.log(0.2), math.log(2.0)))
    cell_scale = jnp.exp(jax.random.uniform(third, (1, 1, ROWS, COLS), jnp.float32, math.log(0.2), math.log(2.0)))
    frame_scale = jnp.exp(math.log(0.001) + math.log(1000.0) * frame_pos).reshape(FRAMES, 1, 1, 1)
    base = jnp.clip(jax.random.normal(first, (FRAMES, CH, ROWS, COLS), jnp.float32), -4.0, 4.0)
    values = base * chan_scale * cell_scale * frame_scale
    return values.astype(jnp.bfloat16)


def spiked(array, stream_key, source, target, blocks, factor):
    owner, partner = [(jnp.arange(array.shape[position]) // (array.shape[position] // blocks)).reshape([-1 if axis == position else 1 for axis in range(array.ndim)]) for position in (source, target)]
    chosen = jax.random.permutation(stream_key, blocks)[partner]
    strong = (owner == chosen) | (owner == (partner + blocks // 2) % blocks)
    return jnp.where(strong, factor * array, array)


def shard_levels(rng, dims, pieces, smallest, top_value):
    gain = 1.0
    for dim, parts in pieces:
        heights = jax.random.uniform(jax.random.fold_in(jax.random.fold_in(rng, 6), dim), (parts,), jnp.float32, smallest / len(pieces), top_value / len(pieces))
        gain = gain * jnp.repeat(jnp.exp(heights), dims[dim] // parts).reshape((-1,) + (1,) * (len(dims) - 1 - dim))
    return gain


def heavy_noise(own_key, shape, width, limit, pieces, heavy, kind=jnp.bfloat16):
    result = width * jax.random.normal(own_key, shape, jnp.float32)
    if pieces:
        result = result * shard_levels(own_key, shape, pieces, -0.22, 0.18)
    return jnp.clip(spiked(result, jax.random.fold_in(own_key, 3), *heavy), -limit, limit).astype(kind)


def setup_inputs(seed: int = 0) -> dict:
    streams_of = jax.random.split(jax.random.key(seed), 5)
    latents = draw_latents(jax.random.fold_in(streams_of[4], 71), 0)
    spatial_weight = heavy_noise(streams_of[1], (3, 3, CH, CH), (9 * CH) ** -0.5, 0.078125, ((2, 4),), (2, 3, 4, 2.0))
    temporal_weight = heavy_noise(streams_of[2], (3, CH, CH), (3 * CH) ** -0.5, 0.125, ((1, 4),), (1, 2, 4, 2.0))
    mix_factor = jnp.clip(jax.random.uniform(streams_of[3], (1,), jnp.float32, -1.5, 1.5), -1.5, 1.5)
    return dict(latents=latents, spatial_weight=spatial_weight, temporal_weight=temporal_weight, mix_factor=mix_factor)


norm_eps = 1e-05

def group_norm_silu(values, axes):
    group_mean = lax.optimization_barrier(jnp.mean(values, axis=axes, keepdims=True))
    squares = lax.optimization_barrier(jnp.mean(values * values, axis=axes, keepdims=True))
    group_var = squares - group_mean * group_mean
    return jax.nn.silu((values - group_mean) * lax.rsqrt(group_var + norm_eps))

def spatial_frame(frame_act, spatial_weight):
    channels, height, columns = frame_act.shape
    padded = jnp.pad(frame_act, ((0, 0), (1, 1), (1, 1)))
    running = jnp.zeros((channels, height * columns), jnp.float32)
    for row_tap in range(3):
        for col_tap in range(3):
            shifted = padded[:, row_tap:row_tap + height, col_tap:col_tap + columns].reshape(channels, height * columns)
            running = running + jnp.dot(spatial_weight[row_tap, col_tap].T, shifted, preferred_element_type=jnp.float32)
    return running.reshape(channels, height, columns)

def reference(latents, spatial_weight, temporal_weight, mix_factor):
    latents_f = latents.astype(jnp.float32)
    frames, channels, height, columns = latents_f.shape
    grouped = latents_f.reshape(frames, GROUPS, channels // GROUPS, height * columns)
    act_spatial = group_norm_silu(grouped, (2, 3)).reshape(frames, channels, height, columns).astype(jnp.bfloat16)
    spatial = lax.map(lambda frame_act: spatial_frame(frame_act, spatial_weight), act_spatial)
    hidden = latents_f + spatial
    grouped = hidden.reshape(frames, GROUPS, channels // GROUPS, height * columns)
    act_temporal = group_norm_silu(grouped, (0, 2, 3)).reshape(frames, channels, height * columns).astype(jnp.bfloat16)
    padded = jnp.pad(act_temporal, ((1, 1), (0, 0), (0, 0)))

    def temporal_frame(frame_index):
        window = lax.dynamic_slice_in_dim(padded, frame_index, 3, 0)
        running = jnp.zeros((channels, height * columns), jnp.float32)
        for time_tap in range(3):
            running = running + jnp.dot(temporal_weight[time_tap].T, window[time_tap], preferred_element_type=jnp.float32)
        return running.astype(jnp.bfloat16)
    branch = lax.map(temporal_frame, jnp.arange(frames, dtype=jnp.int32))
    blend_weight = jax.nn.sigmoid(mix_factor[0])
    mixed_out = hidden + (1.0 - blend_weight) * branch.astype(jnp.float32).reshape(frames, channels, height, columns)
    return mixed_out.astype(jnp.bfloat16)
```

```python
import functools

import jax
import jax.numpy as jnp
from jax import lax
from jax.experimental import pallas as pl
from jax.experimental.pallas import tpu as pltpu
from jax.sharding import PartitionSpec as P

CH = 1280
GROUPS = 32
GROUP = CH // GROUPS
ROWS = 16
COLS = 32
PX = ROWS * COLS
LOCAL = CH // 4
LOCAL_GROUPS = LOCAL // GROUP
TAPS = 3
WIDE = TAPS * LOCAL
TILE = 256
EPS = 1e-05

CORE_SWAP = [(0, 1), (1, 0), (2, 3), (3, 2)]
HALF_SWAP = [(0, 2), (2, 0), (1, 3), (3, 1)]
VMEM_LIMIT = 40 * 1024 * 1024
BF16 = jnp.bfloat16
F32 = jnp.float32
HIGHEST = lax.Precision.HIGHEST


def params():
    return pltpu.CompilerParams(vmem_limit_bytes=VMEM_LIMIT)


def silu(v):
    half = 0.5 * v
    return half + half * jnp.tanh(half)


def group_block():
    row = lax.broadcasted_iota(jnp.int32, (LOCAL, LOCAL), 0)
    col = lax.broadcasted_iota(jnp.int32, (LOCAL, LOCAL), 1)
    out = jnp.zeros((LOCAL, LOCAL), F32)
    for g in range(LOCAL_GROUPS):
        lo, hi = g * GROUP, (g + 1) * GROUP
        same = (row >= lo) & (row < hi) & (col >= lo) & (col < hi)
        out = jnp.where(same, 1.0, out)
    return out


def group_to_lane(shift):
    row = lax.broadcasted_iota(jnp.int32, (LOCAL, 128), 0)
    lane = lax.broadcasted_iota(jnp.int32, (LOCAL, 128), 1) - shift
    return jnp.where((row >= lane * GROUP) & (row < (lane + 1) * GROUP), 1.0, 0.0)


def lane_to_group(shift):
    lane = lax.broadcasted_iota(jnp.int32, (128, LOCAL), 0) - shift
    col = lax.broadcasted_iota(jnp.int32, (128, LOCAL), 1)
    return jnp.where((col >= lane * GROUP) & (col < (lane + 1) * GROUP), 1.0, 0.0)


def exact_dot(a, b):
    return jnp.dot(a, b, precision=HIGHEST, preferred_element_type=F32)


def pack(block):
    return jnp.concatenate([block[: PX // 2], block[PX // 2 :]], axis=1)


def unpack(ref):
    return jnp.concatenate([ref[:, :LOCAL], ref[:, LOCAL:]], axis=0)


def split_cores(total_ref, send_ref, own_ref):
    core = lax.axis_index("ch") % 2

    def copy(ref, first):
        ref[:, :LOCAL] = total_ref[:, first : first + LOCAL]
        ref[:, LOCAL:] = total_ref[:, first + 2 * LOCAL : first + 3 * LOCAL]

    @pl.when(core == 0)
    def _():
        copy(own_ref, 0)
        copy(send_ref, LOCAL)

    @pl.when(core == 1)
    def _():
        copy(own_ref, LOCAL)
        copy(send_ref, 0)


def spatial_kernel(lat_ref, weight_ref, send_ref, own_ref, taps_ref, total_ref):
    tile = pl.program_id(0)

    @pl.when(tile == 0)
    def _():
        lat = lat_ref[...].astype(F32)
        sums = jnp.sum(lat, axis=0, keepdims=True)
        squares = jnp.sum(lat * lat, axis=0, keepdims=True)
        both = jnp.concatenate([sums, squares, jnp.zeros((6, LOCAL), F32)], axis=0)
        both = exact_dot(both, group_block()) * (1.0 / (GROUP * PX))
        mean = both[0:1]
        var = both[1:2] - mean * mean
        act = silu((lat - mean) * lax.rsqrt(var + EPS))
        col = lax.broadcasted_iota(jnp.int32, (PX, LOCAL), 0) % COLS
        left = jnp.where(col == 0, 0.0, pltpu.roll(act, 1, 0))
        right = jnp.where(col == COLS - 1, 0.0, pltpu.roll(act, PX - 1, 0))
        taps_ref[:COLS, :] = jnp.zeros((COLS, WIDE), BF16)
        taps_ref[COLS + PX :, :] = jnp.zeros((COLS, WIDE), BF16)
        taps_ref[COLS : COLS + PX, :] = jnp.concatenate([left, act, right], axis=1).astype(BF16)

    total = None
    for row_tap in range(TAPS):
        term = jnp.dot(
            taps_ref[row_tap * COLS : row_tap * COLS + PX, :],
            weight_ref[row_tap],
            preferred_element_type=F32,
        )
        total = term if total is None else total + term
    total_ref[:, pl.ds(pl.multiple_of(tile * TILE, TILE), TILE)] = total.astype(BF16)

    @pl.when(tile == CH // TILE - 1)
    def _():
        split_cores(total_ref, send_ref, own_ref)


def spatial_call(lat, weight, frame):
    shape = jax.ShapeDtypeStruct((PX, 2 * LOCAL), BF16)
    return pl.pallas_call(
        spatial_kernel,
        grid=(CH // TILE,),
        in_specs=[
            pl.BlockSpec((PX, LOCAL), lambda n: (frame, 0)),
            pl.BlockSpec((TAPS, WIDE, TILE), lambda n: (0, 0, n)),
        ],
        out_specs=[pl.BlockSpec((PX, 2 * LOCAL), lambda n: (0, 0))] * 2,
        out_shape=[shape, shape],
        scratch_shapes=[
            pltpu.VMEM((PX + 2 * COLS, WIDE), BF16),
            pltpu.VMEM((PX, CH), BF16),
        ],
        compiler_params=params(),
        cost_estimate=pl.CostEstimate(
            flops=2 * PX * TAPS * WIDE * CH,
            bytes_accessed=2 * TAPS * WIDE * CH,
            transcendentals=PX * LOCAL,
        ),
        name="spatial",
    )(lat, weight)


def temporal_kernel(last, hidden_ref, halo_ref, stats_ref, weight_ref, send_ref, own_ref, taps_ref, total_ref):
    tile = pl.program_id(0)

    @pl.when(tile == 0)
    def _():
        seq, size = lax.axis_index("seq"), lax.axis_size("seq")
        sums = jnp.sum(stats_ref[...], axis=0, keepdims=True) * (1.0 / (GROUP * 2 * PX * size))
        sums = jnp.broadcast_to(sums, (8, 128))
        mean = exact_dot(sums, lane_to_group(0))[0:1]
        var = exact_dot(sums, lane_to_group(LOCAL_GROUPS))[0:1] - mean * mean
        scale = lax.rsqrt(var + EPS)

        def act(values):
            return silu((values - mean) * scale)

        edge = (seq == size - 1) if last else (seq == 0)
        halo = act(unpack(halo_ref).astype(F32)) * jnp.where(edge, 0.0, 1.0)
        first, second = act(hidden_ref[:PX]), act(hidden_ref[PX:])
        frames = [first, second, halo] if last else [halo, first, second]
        taps_ref[...] = jnp.concatenate(frames, axis=1).astype(BF16)

    total = jnp.dot(taps_ref[...], weight_ref[...], preferred_element_type=F32)
    total_ref[:, pl.ds(pl.multiple_of(tile * TILE, TILE), TILE)] = total.astype(BF16)

    @pl.when(tile == CH // TILE - 1)
    def _():
        split_cores(total_ref, send_ref, own_ref)


def temporal_call(hidden, halo, stats, weight, last):
    shape = jax.ShapeDtypeStruct((PX, 2 * LOCAL), BF16)
    return pl.pallas_call(
        functools.partial(temporal_kernel, last),
        grid=(CH // TILE,),
        in_specs=[
            pl.BlockSpec(hidden.shape, lambda n: (0, 0)),
            pl.BlockSpec(halo.shape, lambda n: (0, 0)),
            pl.BlockSpec(stats.shape, lambda n: (0, 0)),
            pl.BlockSpec((WIDE, TILE), lambda n: (0, n)),
        ],
        out_specs=[pl.BlockSpec((PX, 2 * LOCAL), lambda n: (0, 0))] * 2,
        out_shape=[shape, shape],
        scratch_shapes=[
            pltpu.VMEM((PX, WIDE), BF16),
            pltpu.VMEM((PX, CH), BF16),
        ],
        compiler_params=params(),
        cost_estimate=pl.CostEstimate(
            flops=2 * PX * WIDE * CH,
            bytes_accessed=2 * WIDE * CH,
            transcendentals=3 * PX * LOCAL,
        ),
        name="temporal",
    )(hidden, halo, stats, weight)


def chip_sum_kernel(own_ref, got_ref, send_ref, keep_ref):
    half = lax.axis_index("ch") // 2

    def block(first):
        cols = slice(first, first + LOCAL)
        return own_ref[:, cols].astype(F32) + got_ref[:, cols].astype(F32)

    @pl.when(half == 0)
    def _():
        keep_ref[...] = block(0)
        send_ref[...] = pack(block(LOCAL)).astype(BF16)

    @pl.when(half == 1)
    def _():
        keep_ref[...] = block(LOCAL)
        send_ref[...] = pack(block(0)).astype(BF16)


def chip_sum(own, got):
    return pl.pallas_call(
        chip_sum_kernel,
        out_shape=[
            jax.ShapeDtypeStruct((PX // 2, 2 * LOCAL), BF16),
            jax.ShapeDtypeStruct((PX, LOCAL), F32),
        ],
        compiler_params=params(),
        cost_estimate=pl.CostEstimate(flops=PX * 2 * LOCAL, bytes_accessed=8 * PX * LOCAL, transcendentals=0),
        name="chip_sum",
    )(own, got)


def hidden_kernel(lat_ref, keep0, keep1, got0, got1, hidden_ref, first_ref, last_ref, stats_ref):
    sums, squares = 0.0, 0.0
    for frame, (keep, got, edge) in enumerate(((keep0, got0, first_ref), (keep1, got1, last_ref))):
        cells = slice(frame * PX, (frame + 1) * PX)
        hidden = lat_ref[cells].astype(F32) + keep[...] + unpack(got).astype(F32)
        hidden_ref[cells] = hidden
        edge[...] = pack(hidden).astype(BF16)
        sums += jnp.sum(hidden, axis=0, keepdims=True)
        squares += jnp.sum(hidden * hidden, axis=0, keepdims=True)
    row = exact_dot(jnp.broadcast_to(sums, (8, LOCAL)), group_to_lane(0))
    row += exact_dot(jnp.broadcast_to(squares, (8, LOCAL)), group_to_lane(LOCAL_GROUPS))
    stats_ref[...] = jnp.broadcast_to(row[0:1], stats_ref.shape)


def hidden_call(lat, keeps, gots, size):
    edge = jax.ShapeDtypeStruct((PX // 2, 2 * LOCAL), BF16)
    return pl.pallas_call(
        hidden_kernel,
        out_shape=[
            jax.ShapeDtypeStruct((2 * PX, LOCAL), F32),
            edge,
            edge,
            jax.ShapeDtypeStruct((size, 128), F32),
        ],
        compiler_params=params(),
        cost_estimate=pl.CostEstimate(flops=10 * PX * LOCAL, bytes_accessed=20 * PX * LOCAL, transcendentals=0),
        name="hidden",
    )(lat, *keeps, *gots)


def blend_kernel(mix_ref, hidden_ref, keep0, keep1, got0, got1, out_ref):
    mix = jnp.full((1, LOCAL), mix_ref[0], F32)
    weight = 1.0 - jax.nn.sigmoid(mix)
    for frame, (keep, got) in enumerate(((keep0, got0), (keep1, got1))):
        cells = slice(frame * PX, (frame + 1) * PX)
        branch = (keep[...] + unpack(got).astype(F32)).astype(BF16).astype(F32)
        out_ref[cells] = (hidden_ref[cells] + weight * branch).astype(BF16)


def blend_call(mix, hidden, keeps, gots):
    whole = pl.BlockSpec(memory_space=pltpu.VMEM)
    return pl.pallas_call(
        blend_kernel,
        in_specs=[pl.BlockSpec(memory_space=pltpu.SMEM)] + [whole] * 5,
        out_specs=whole,
        out_shape=jax.ShapeDtypeStruct((2 * PX, LOCAL), BF16),
        compiler_params=params(),
        cost_estimate=pl.CostEstimate(flops=6 * PX * LOCAL, bytes_accessed=16 * PX * LOCAL, transcendentals=0),
        name="blend",
    )(mix, hidden, *keeps, *gots)


def reduce_channels(parts):
    keeps, gots = [], []
    for send, own in parts:
        got = lax.ppermute(send, "ch", CORE_SWAP)
        send, keep = chip_sum(own, got)
        keeps.append(keep)
        gots.append(lax.ppermute(send, "ch", HALF_SWAP))
    return keeps, gots


def per_device(latents, spatial_weight, temporal_weight, mix_factor):
    size = lax.axis_size("seq")
    lat = latents.transpose(0, 2, 3, 1).reshape(2 * PX, LOCAL)
    weight_s = spatial_weight.reshape(TAPS, WIDE, CH)
    weight_t = temporal_weight.reshape(WIDE, CH)
    keeps, gots = reduce_channels([spatial_call(lat, weight_s, frame) for frame in range(2)])
    hidden, first, last, stats = hidden_call(lat, keeps, gots, size)
    after = lax.ppermute(first, "seq", [(i + 1, i) for i in range(size - 1)])
    before = lax.ppermute(last, "seq", [(i, i + 1) for i in range(size - 1)])
    stats = lax.all_to_all(stats, "seq", 0, 0, tiled=True)
    keeps, gots = reduce_channels(
        [
            temporal_call(hidden, before, stats, weight_t, False),
            temporal_call(hidden, after, stats, weight_t, True),
        ]
    )
    out = blend_call(mix_factor, hidden, keeps, gots)
    return out.reshape(2, ROWS, COLS, LOCAL).transpose(0, 3, 1, 2)


def solution(mesh):
    placed = (P("seq", "ch", None, None), P(None, None, "ch", None), P(None, "ch", None), P())
    return jax.shard_map(
        per_device,
        mesh=mesh,
        in_specs=placed,
        out_specs=P("seq", "ch", None, None),
        check_vma=False,
    )
```

```python
import functools

import jax
import jax.numpy as jnp
from jax import lax
from jax.experimental import pallas as pl
from jax.experimental.pallas import tpu as pltpu
from jax.sharding import PartitionSpec as P

CH = 1280
GROUPS = 32
GROUP = CH // GROUPS
ROWS = 16
COLS = 32
PX = ROWS * COLS
LOCAL = CH // 4
LOCAL_GROUPS = LOCAL // GROUP
TAPS = 3
WIDE = TAPS * LOCAL
HALF = CH // 2
EPS = 1e-05

CORE_SWAP = [(0, 1), (1, 0), (2, 3), (3, 2)]
HALF_SWAP = [(0, 2), (2, 0), (1, 3), (3, 1)]
CORE_PIECES = 2
HALF_PIECES = 1
VMEM_LIMIT = 40 * 1024 * 1024
BF16 = jnp.bfloat16
F32 = jnp.float32
HIGHEST = lax.Precision.HIGHEST


def params():
    return pltpu.CompilerParams(vmem_limit_bytes=VMEM_LIMIT)


def silu(v):
    half = 0.5 * v
    return half + half * jnp.tanh(half)


def group_of(channel):
    return (channel * 205) >> 13


def group_block():
    row = lax.broadcasted_iota(jnp.int32, (LOCAL, LOCAL), 0)
    col = lax.broadcasted_iota(jnp.int32, (LOCAL, LOCAL), 1)
    return jnp.where(group_of(row) == group_of(col), 1.0, 0.0)


def group_to_lane(shift):
    row = lax.broadcasted_iota(jnp.int32, (LOCAL, 128), 0)
    lane = lax.broadcasted_iota(jnp.int32, (LOCAL, 128), 1)
    return jnp.where(group_of(row) == lane - shift, 1.0, 0.0)


def lane_to_group(shift):
    lane = lax.broadcasted_iota(jnp.int32, (128, LOCAL), 0)
    col = lax.broadcasted_iota(jnp.int32, (128, LOCAL), 1)
    return jnp.where(group_of(col) == lane - shift, 1.0, 0.0)


def exact_dot(a, b):
    return jnp.dot(a, b, precision=HIGHEST, preferred_element_type=F32)


def pack(block):
    return jnp.concatenate([block[: PX // 2], block[PX // 2 :]], axis=1)


def unpack(ref):
    return jnp.concatenate([ref[:, :LOCAL], ref[:, LOCAL:]], axis=0)


def split_cores(total_ref, send_ref, own_ref):
    core = lax.axis_index("ch") % 2

    def copy(ref, first):
        for frame in range(2):
            ref[:, frame * LOCAL : (frame + 1) * LOCAL] = total_ref[frame, :, first : first + LOCAL]

    @pl.when(core == 0)
    def _():
        copy(own_ref, 0)
        copy(send_ref, LOCAL)

    @pl.when(core == 1)
    def _():
        copy(own_ref, LOCAL)
        copy(send_ref, 0)


def half_columns(other):
    half = lax.axis_index("ch") // 2
    half = 1 - half if other else half
    return pl.ds(pl.multiple_of(half * HALF, HALF), HALF)


def spatial_kernel(other, lat_hbm, weight_hbm, after_ref, send_ref, own_ref, lat_ref, weight_ref, taps_ref, total_ref, sems):
    copies = [pltpu.make_async_copy(lat_hbm, lat_ref, sems.at[TAPS])]
    for row_tap in range(TAPS):
        source = weight_hbm.at[row_tap, :, half_columns(other)]
        copies.append(pltpu.make_async_copy(source, weight_ref.at[row_tap], sems.at[row_tap]))
    for copy in copies:
        copy.start()
    copies[0].wait()

    rows = []
    for frame in range(2):
        lat = lat_ref[frame * PX : (frame + 1) * PX].astype(F32)
        rows.append(jnp.sum(lat, axis=0, keepdims=True))
        rows.append(jnp.sum(lat * lat, axis=0, keepdims=True))
    means = jnp.concatenate(rows + [jnp.zeros((4, LOCAL), F32)], axis=0)
    means = exact_dot(means, group_block()) * (1.0 / (GROUP * PX))
    col = lax.broadcasted_iota(jnp.int32, (COLS, LOCAL), 0)
    for frame in range(2):
        mean = means[2 * frame : 2 * frame + 1]
        var = means[2 * frame + 1 : 2 * frame + 2] - mean * mean
        lat = lat_ref[frame * PX : (frame + 1) * PX].astype(F32)
        act = silu((lat - mean) * lax.rsqrt(var + EPS))
        left, right = [], []
        for row in range(ROWS):
            cells = act[row * COLS : (row + 1) * COLS]
            left.append(jnp.where(col == 0, 0.0, pltpu.roll(cells, 1, 0)))
            right.append(jnp.where(col == COLS - 1, 0.0, pltpu.roll(cells, COLS - 1, 0)))
        taps_ref[frame, :COLS] = jnp.zeros((COLS, WIDE), BF16)
        taps_ref[frame, COLS + PX :] = jnp.zeros((COLS, WIDE), BF16)
        inside = slice(COLS, COLS + PX)
        taps_ref[frame, inside, :LOCAL] = jnp.concatenate(left, axis=0).astype(BF16)
        taps_ref[frame, inside, LOCAL : 2 * LOCAL] = act.astype(BF16)
        taps_ref[frame, inside, 2 * LOCAL :] = jnp.concatenate(right, axis=0).astype(BF16)

    for copy in copies[1:]:
        copy.wait()
    for frame in range(2):
        total = None
        for row_tap in range(TAPS):
            cells = slice(row_tap * COLS, row_tap * COLS + PX)
            term = jnp.dot(taps_ref[frame, cells], weight_ref[row_tap], preferred_element_type=F32)
            total = term if total is None else total + term
        total_ref[frame] = total.astype(BF16)
    split_cores(total_ref, send_ref, own_ref)


def spatial_call(lat, weight, after, other):
    shape = jax.ShapeDtypeStruct((PX, 2 * LOCAL), BF16)
    vmem, hbm = pl.BlockSpec(memory_space=pltpu.VMEM), pl.BlockSpec(memory_space=pltpu.HBM)
    return pl.pallas_call(
        functools.partial(spatial_kernel, other),
        in_specs=[hbm, hbm, pl.BlockSpec(memory_space=pl.ANY)],
        out_specs=[vmem, vmem],
        out_shape=[shape, shape],
        scratch_shapes=[
            pltpu.VMEM((2 * PX, LOCAL), BF16),
            pltpu.VMEM((TAPS, WIDE, HALF), BF16),
            pltpu.VMEM((2, PX + 2 * COLS, WIDE), BF16),
            pltpu.VMEM((2, PX, HALF), BF16),
            pltpu.SemaphoreType.DMA((TAPS + 1,)),
        ],
        compiler_params=params(),
        cost_estimate=pl.CostEstimate(
            flops=4 * PX * TAPS * WIDE * HALF,
            bytes_accessed=2 * TAPS * WIDE * HALF,
            transcendentals=2 * PX * LOCAL,
        ),
        name="spatial",
    )(lat, weight, after)


def temporal_kernel(
    other, hidden_ref, before_ref, next_ref, stats_ref, weight_hbm, after_ref, send_ref, own_ref, weight_ref, taps_ref, total_ref, sem
):
    copy = pltpu.make_async_copy(weight_hbm.at[:, half_columns(other)], weight_ref, sem)
    copy.start()
    seq, size = lax.axis_index("seq"), lax.axis_size("seq")
    sums = jnp.sum(stats_ref[...], axis=0, keepdims=True) * (1.0 / (GROUP * 2 * PX * size))
    sums = jnp.broadcast_to(sums, (8, 128))
    mean = exact_dot(sums, lane_to_group(0))[0:1]
    var = exact_dot(sums, lane_to_group(LOCAL_GROUPS))[0:1] - mean * mean
    scale = lax.rsqrt(var + EPS)

    def act(values):
        return silu((values - mean) * scale)

    before = act(unpack(before_ref).astype(F32)) * jnp.where(seq == 0, 0.0, 1.0)
    after = act(unpack(next_ref).astype(F32)) * jnp.where(seq == size - 1, 0.0, 1.0)
    frames = [before, act(hidden_ref[:PX]), act(hidden_ref[PX:]), after]
    for frame in range(2):
        for tap in range(TAPS):
            taps_ref[frame, :, tap * LOCAL : (tap + 1) * LOCAL] = frames[frame + tap].astype(BF16)
    copy.wait()
    for frame in range(2):
        total_ref[frame] = jnp.dot(taps_ref[frame], weight_ref[...], preferred_element_type=F32).astype(BF16)
    split_cores(total_ref, send_ref, own_ref)


def temporal_call(hidden, before, next_, stats, weight, after, other):
    shape = jax.ShapeDtypeStruct((PX, 2 * LOCAL), BF16)
    vmem = pl.BlockSpec(memory_space=pltpu.VMEM)
    return pl.pallas_call(
        functools.partial(temporal_kernel, other),
        in_specs=[vmem] * 4 + [pl.BlockSpec(memory_space=pl.ANY)] * 2,
        out_specs=[vmem, vmem],
        out_shape=[shape, shape],
        scratch_shapes=[
            pltpu.VMEM((WIDE, HALF), BF16),
            pltpu.VMEM((2, PX, WIDE), BF16),
            pltpu.VMEM((2, PX, HALF), BF16),
            pltpu.SemaphoreType.DMA,
        ],
        compiler_params=params(),
        cost_estimate=pl.CostEstimate(
            flops=4 * PX * WIDE * HALF,
            bytes_accessed=2 * WIDE * HALF,
            transcendentals=4 * PX * LOCAL,
        ),
        name="temporal",
    )(hidden, before, next_, stats, weight, after)


def chip_sum_kernel(own_ref, got_ref, out_ref):
    out_ref[...] = (own_ref[...].astype(F32) + got_ref[...].astype(F32)).astype(BF16)


def chip_sum(own, got):
    return pl.pallas_call(
        chip_sum_kernel,
        out_shape=jax.ShapeDtypeStruct((PX, 2 * LOCAL), BF16),
        compiler_params=params(),
        cost_estimate=pl.CostEstimate(flops=2 * PX * LOCAL, bytes_accessed=12 * PX * LOCAL, transcendentals=0),
        name="chip_sum",
    )(own, got)


def three_sums(own_ref, core_refs, half_refs, frame):
    cols = slice(frame * LOCAL, (frame + 1) * LOCAL)
    core = jnp.concatenate([ref[:, cols] for ref in core_refs], axis=0)
    half = jnp.concatenate([ref[:, cols] for ref in half_refs], axis=0)
    return own_ref[:, cols].astype(F32) + core.astype(F32) + half.astype(F32)


def hidden_kernel(lat_ref, own_ref, *refs):
    cores, halves = refs[:CORE_PIECES], refs[CORE_PIECES : CORE_PIECES + HALF_PIECES]
    hidden_ref, first_ref, last_ref, stats_ref = refs[CORE_PIECES + HALF_PIECES :]
    sums, squares = 0.0, 0.0
    for frame, edge in enumerate((first_ref, last_ref)):
        cells = slice(frame * PX, (frame + 1) * PX)
        hidden = lat_ref[cells].astype(F32) + three_sums(own_ref, cores, halves, frame)
        hidden_ref[cells] = hidden
        edge[...] = pack(hidden).astype(BF16)
        sums += jnp.sum(hidden, axis=0, keepdims=True)
        squares += jnp.sum(hidden * hidden, axis=0, keepdims=True)
    row = exact_dot(jnp.broadcast_to(sums, (8, LOCAL)), group_to_lane(0))
    row += exact_dot(jnp.broadcast_to(squares, (8, LOCAL)), group_to_lane(LOCAL_GROUPS))
    stats_ref[...] = jnp.broadcast_to(row[0:1], stats_ref.shape)


def hidden_call(lat, shares, size):
    edge = jax.ShapeDtypeStruct((PX // 2, 2 * LOCAL), BF16)
    return pl.pallas_call(
        hidden_kernel,
        out_shape=[
            jax.ShapeDtypeStruct((2 * PX, LOCAL), F32),
            edge,
            edge,
            jax.ShapeDtypeStruct((size, 128), F32),
        ],
        compiler_params=params(),
        cost_estimate=pl.CostEstimate(flops=10 * PX * LOCAL, bytes_accessed=20 * PX * LOCAL, transcendentals=0),
        name="hidden",
    )(lat, *shares)


def blend_kernel(mix_ref, hidden_ref, own_ref, *refs):
    cores, halves, out_ref = refs[:CORE_PIECES], refs[CORE_PIECES:-1], refs[-1]
    mix = jnp.full((1, LOCAL), mix_ref[0], F32)
    weight = 1.0 - jax.nn.sigmoid(mix)
    for frame in range(2):
        cells = slice(frame * PX, (frame + 1) * PX)
        branch = three_sums(own_ref, cores, halves, frame).astype(BF16).astype(F32)
        out_ref[cells] = (hidden_ref[cells] + weight * branch).astype(BF16)


def blend_call(mix, hidden, shares):
    whole = pl.BlockSpec(memory_space=pltpu.VMEM)
    return pl.pallas_call(
        blend_kernel,
        in_specs=[pl.BlockSpec(memory_space=pltpu.SMEM)] + [whole] * (2 + CORE_PIECES + HALF_PIECES),
        out_specs=whole,
        out_shape=jax.ShapeDtypeStruct((2 * PX, LOCAL), BF16),
        compiler_params=params(),
        cost_estimate=pl.CostEstimate(flops=6 * PX * LOCAL, bytes_accessed=16 * PX * LOCAL, transcendentals=0),
        name="blend",
    )(mix, hidden, *shares)


def permute(array, perm, pieces):
    rows = array.shape[0] // pieces
    return [lax.ppermute(array[i * rows : (i + 1) * rows], "ch", perm) for i in range(pieces)]


def reduce_channels(conv, after):
    send, own = conv(after, True)
    chip = chip_sum(own, permute(send, CORE_SWAP, 1)[0])
    halves = permute(chip, HALF_SWAP, HALF_PIECES)
    send, own = conv(chip, False)
    return own, *permute(send, CORE_SWAP, CORE_PIECES), *halves


def per_device(latents, spatial_weight, temporal_weight, mix_factor):
    size = lax.axis_size("seq")
    lat = latents.transpose(0, 2, 3, 1).reshape(2 * PX, LOCAL)
    lat_hbm = pltpu.with_memory_space_constraint(lat, pltpu.HBM)
    weight_s = pltpu.with_memory_space_constraint(spatial_weight.reshape(TAPS, WIDE, CH), pltpu.HBM)
    weight_t = temporal_weight.reshape(WIDE, CH)
    shares = reduce_channels(functools.partial(spatial_call, lat_hbm, weight_s), lat_hbm)
    hidden, first, last, stats = hidden_call(lat, shares, size)
    next_ = lax.ppermute(first, "seq", [(i + 1, i) for i in range(size - 1)])
    before = lax.ppermute(last, "seq", [(i, i + 1) for i in range(size - 1)])
    stats = lax.all_to_all(stats, "seq", 0, 0, tiled=True)
    shares = reduce_channels(functools.partial(temporal_call, hidden, before, next_, stats, weight_t), hidden)
    out = blend_call(mix_factor, hidden, shares)
    return out.reshape(2, ROWS, COLS, LOCAL).transpose(0, 3, 1, 2)


def solution(mesh):
    placed = (P("seq", "ch", None, None), P(None, None, "ch", None), P(None, "ch", None), P())
    return jax.shard_map(
        per_device,
        mesh=mesh,
        in_specs=placed,
        out_specs=P("seq", "ch", None, None),
        check_vma=False,
    )
```

```python
import functools

import jax
import jax.numpy as jnp
from jax import lax
from jax.experimental import pallas as pl
from jax.experimental.pallas import tpu as pltpu
from jax.sharding import PartitionSpec as P

CH = 1280
GROUPS = 32
GROUP = CH // GROUPS
ROWS = 16
COLS = 32
PX = ROWS * COLS
LOCAL = CH // 4
LOCAL_GROUPS = LOCAL // GROUP
TAPS = 3
WIDE = TAPS * LOCAL
HALF = CH // 2
EPS = 1e-05

CORE_SWAP = [(0, 1), (1, 0), (2, 3), (3, 2)]
HALF_SWAP = [(0, 2), (2, 0), (1, 3), (3, 1)]
FIRST = 256
REST = LOCAL - FIRST
CORE_PIECES = 2
VMEM_LIMIT = 40 * 1024 * 1024
BF16 = jnp.bfloat16
F32 = jnp.float32
HIGHEST = lax.Precision.HIGHEST


def params():
    return pltpu.CompilerParams(vmem_limit_bytes=VMEM_LIMIT)


def silu(v):
    half = 0.5 * v
    return half + half * jnp.tanh(half)


def group_of(channel):
    return (channel * 205) >> 13


def group_block():
    row = lax.broadcasted_iota(jnp.int32, (LOCAL, LOCAL), 0)
    col = lax.broadcasted_iota(jnp.int32, (LOCAL, LOCAL), 1)
    return jnp.where(group_of(row) == group_of(col), 1.0, 0.0)


def group_to_lane(shift):
    row = lax.broadcasted_iota(jnp.int32, (LOCAL, 128), 0)
    lane = lax.broadcasted_iota(jnp.int32, (LOCAL, 128), 1)
    return jnp.where(group_of(row) == lane - shift, 1.0, 0.0)


def lane_to_group(shift):
    lane = lax.broadcasted_iota(jnp.int32, (128, LOCAL), 0)
    col = lax.broadcasted_iota(jnp.int32, (128, LOCAL), 1)
    return jnp.where(group_of(col) == lane - shift, 1.0, 0.0)


def exact_dot(a, b):
    return jnp.dot(a, b, precision=HIGHEST, preferred_element_type=F32)


def pack(block):
    return jnp.concatenate([block[: PX // 2], block[PX // 2 :]], axis=1)


def unpack(ref):
    return jnp.concatenate([ref[:, :LOCAL], ref[:, LOCAL:]], axis=0)


def copy_columns(other, weight_hbm, weight_ref, sems):
    half = lax.axis_index("ch") // 2
    away, home = (1 - half) * HALF, half * HALF
    if other:
        pieces = [(away, 0, FIRST), (away + HALF - FIRST, FIRST, FIRST)]
    else:
        pieces = [(away + FIRST, 0, 2 * REST), (home, 2 * REST, HALF)]
    copies = []
    for tap in range(weight_hbm.shape[0]):
        copies.append([])
        for i, (start, to, width) in enumerate(pieces):
            source = weight_hbm.at[tap, :, pl.ds(pl.multiple_of(start, 128), width)]
            copy = pltpu.make_async_copy(source, weight_ref.at[tap, :, to : to + width], sems.at[tap, i])
            copy.start()
            copies[-1].append(copy)
    return copies


def split_first(total_ref, send_ref, own_ref):
    core = lax.axis_index("ch") % 2

    def copy(ref, first):
        for frame in range(2):
            ref[frame * PX : (frame + 1) * PX] = total_ref[frame, :, first : first + FIRST]

    @pl.when(core == 0)
    def _():
        copy(own_ref, 0)
        copy(send_ref, FIRST)

    @pl.when(core == 1)
    def _():
        copy(own_ref, FIRST)
        copy(send_ref, 0)


def split_second(total_ref, send_rest, own_rest, send_ref, own_ref):
    core = lax.axis_index("ch") % 2

    def copy(ref, first, width):
        for frame in range(2):
            ref[:, frame * width : (frame + 1) * width] = total_ref[frame, :, first : first + width]

    @pl.when(core == 0)
    def _():
        copy(own_rest, 0, REST)
        copy(send_rest, REST, REST)
        copy(own_ref, 2 * REST, LOCAL)
        copy(send_ref, 2 * REST + LOCAL, LOCAL)

    @pl.when(core == 1)
    def _():
        copy(own_rest, REST, REST)
        copy(send_rest, 0, REST)
        copy(own_ref, 2 * REST + LOCAL, LOCAL)
        copy(send_ref, 2 * REST, LOCAL)


def part_shapes(other):
    if other:
        return [jax.ShapeDtypeStruct((2 * PX, FIRST), BF16)] * 2
    rest, own = jax.ShapeDtypeStruct((PX, 2 * REST), BF16), jax.ShapeDtypeStruct((PX, 2 * LOCAL), BF16)
    return [rest, rest, own, own]


def part_columns(other):
    return 2 * FIRST if other else 2 * REST + HALF


def spatial_kernel(other, lat_hbm, weight_hbm, after_ref, *refs):
    *outs, lat_ref, weight_ref, taps_ref, total_ref, lat_sem, sems = refs
    lat_copy = pltpu.make_async_copy(lat_hbm, lat_ref, lat_sem)
    lat_copy.start()
    copies = copy_columns(other, weight_hbm, weight_ref, sems)
    lat_copy.wait()

    rows = []
    for frame in range(2):
        lat = lat_ref[frame * PX : (frame + 1) * PX].astype(F32)
        rows.append(jnp.sum(lat, axis=0, keepdims=True))
        rows.append(jnp.sum(lat * lat, axis=0, keepdims=True))
    means = jnp.concatenate(rows + [jnp.zeros((4, LOCAL), F32)], axis=0)
    means = exact_dot(means, group_block()) * (1.0 / (GROUP * PX))
    col = lax.broadcasted_iota(jnp.int32, (COLS, LOCAL), 0)
    for frame in range(2):
        mean = means[2 * frame : 2 * frame + 1]
        var = means[2 * frame + 1 : 2 * frame + 2] - mean * mean
        lat = lat_ref[frame * PX : (frame + 1) * PX].astype(F32)
        act = silu((lat - mean) * lax.rsqrt(var + EPS))
        left, right = [], []
        for row in range(ROWS):
            cells = act[row * COLS : (row + 1) * COLS]
            left.append(jnp.where(col == 0, 0.0, pltpu.roll(cells, 1, 0)))
            right.append(jnp.where(col == COLS - 1, 0.0, pltpu.roll(cells, COLS - 1, 0)))
        taps_ref[frame, :COLS] = jnp.zeros((COLS, WIDE), BF16)
        taps_ref[frame, COLS + PX :] = jnp.zeros((COLS, WIDE), BF16)
        inside = slice(COLS, COLS + PX)
        taps_ref[frame, inside, :LOCAL] = jnp.concatenate(left, axis=0).astype(BF16)
        taps_ref[frame, inside, LOCAL : 2 * LOCAL] = act.astype(BF16)
        taps_ref[frame, inside, 2 * LOCAL :] = jnp.concatenate(right, axis=0).astype(BF16)

    for copy in sum(copies, []):
        copy.wait()
    for frame in range(2):
        total = None
        for row_tap in range(TAPS):
            cells = slice(row_tap * COLS, row_tap * COLS + PX)
            term = jnp.dot(taps_ref[frame, cells], weight_ref[row_tap], preferred_element_type=F32)
            total = term if total is None else total + term
        total_ref[frame] = total.astype(BF16)
    (split_first if other else split_second)(total_ref, *outs)


def spatial_call(lat, weight, after, other):
    vmem, hbm = pl.BlockSpec(memory_space=pltpu.VMEM), pl.BlockSpec(memory_space=pltpu.HBM)
    shapes, columns = part_shapes(other), part_columns(other)
    return pl.pallas_call(
        functools.partial(spatial_kernel, other),
        in_specs=[hbm, hbm, pl.BlockSpec(memory_space=pl.ANY)],
        out_specs=[vmem] * len(shapes),
        out_shape=shapes,
        scratch_shapes=[
            pltpu.VMEM((2 * PX, LOCAL), BF16),
            pltpu.VMEM((TAPS, WIDE, columns), BF16),
            pltpu.VMEM((2, PX + 2 * COLS, WIDE), BF16),
            pltpu.VMEM((2, PX, columns), BF16),
            pltpu.SemaphoreType.DMA,
            pltpu.SemaphoreType.DMA((TAPS, 2)),
        ],
        compiler_params=params(),
        cost_estimate=pl.CostEstimate(
            flops=4 * PX * TAPS * WIDE * columns,
            bytes_accessed=2 * TAPS * WIDE * columns,
            transcendentals=2 * PX * LOCAL,
        ),
        name="spatial",
    )(lat, weight, after)


def temporal_kernel(other, hidden_ref, before_ref, next_ref, stats_ref, weight_hbm, after_ref, *refs):
    *outs, weight_ref, taps_ref, total_ref, sems = refs
    copies = copy_columns(other, weight_hbm, weight_ref, sems)
    seq, size = lax.axis_index("seq"), lax.axis_size("seq")
    sums = jnp.sum(stats_ref[...], axis=0, keepdims=True) * (1.0 / (GROUP * 2 * PX * size))
    sums = jnp.broadcast_to(sums, (8, 128))
    mean = exact_dot(sums, lane_to_group(0))[0:1]
    var = exact_dot(sums, lane_to_group(LOCAL_GROUPS))[0:1] - mean * mean
    scale = lax.rsqrt(var + EPS)

    def act(values):
        return silu((values - mean) * scale)

    before = act(unpack(before_ref).astype(F32)) * jnp.where(seq == 0, 0.0, 1.0)
    after = act(unpack(next_ref).astype(F32)) * jnp.where(seq == size - 1, 0.0, 1.0)
    frames = [before, act(hidden_ref[:PX]), act(hidden_ref[PX:]), after]
    for frame in range(2):
        for tap in range(TAPS):
            taps_ref[frame, :, tap * LOCAL : (tap + 1) * LOCAL] = frames[frame + tap].astype(BF16)
    for copy in copies[0]:
        copy.wait()
    for frame in range(2):
        total_ref[frame] = jnp.dot(taps_ref[frame], weight_ref[0], preferred_element_type=F32).astype(BF16)
    (split_first if other else split_second)(total_ref, *outs)


def temporal_call(hidden, before, next_, stats, weight, after, other):
    vmem = pl.BlockSpec(memory_space=pltpu.VMEM)
    shapes, columns = part_shapes(other), part_columns(other)
    return pl.pallas_call(
        functools.partial(temporal_kernel, other),
        in_specs=[vmem] * 4 + [pl.BlockSpec(memory_space=pl.ANY)] * 2,
        out_specs=[vmem] * len(shapes),
        out_shape=shapes,
        scratch_shapes=[
            pltpu.VMEM((1, WIDE, columns), BF16),
            pltpu.VMEM((2, PX, WIDE), BF16),
            pltpu.VMEM((2, PX, columns), BF16),
            pltpu.SemaphoreType.DMA((1, 2)),
        ],
        compiler_params=params(),
        cost_estimate=pl.CostEstimate(
            flops=4 * PX * WIDE * columns,
            bytes_accessed=2 * WIDE * columns,
            transcendentals=4 * PX * LOCAL,
        ),
        name="temporal",
    )(hidden, before, next_, stats, weight, after)


def chip_sum_kernel(own_ref, got_ref, out_ref):
    out_ref[...] = (own_ref[...].astype(F32) + got_ref[...].astype(F32)).astype(BF16)


def chip_sum(own, got):
    return pl.pallas_call(
        chip_sum_kernel,
        out_shape=jax.ShapeDtypeStruct(own.shape, BF16),
        compiler_params=params(),
        cost_estimate=pl.CostEstimate(flops=own.size, bytes_accessed=6 * own.size, transcendentals=0),
        name="chip_sum",
    )(own, got)


def three_sums(own_ref, core_refs, first_ref, rest_ref, frame):
    cols = slice(frame * LOCAL, (frame + 1) * LOCAL)
    core = jnp.concatenate([ref[:, cols] for ref in core_refs], axis=0)
    first = first_ref[frame * PX : (frame + 1) * PX].astype(F32)
    rest = rest_ref[:, frame * REST : (frame + 1) * REST].astype(F32)
    half = jnp.where(
        lax.axis_index("ch") % 2 == 0,
        jnp.concatenate([first, rest], axis=1),
        jnp.concatenate([rest, first], axis=1),
    )
    return own_ref[:, cols].astype(F32) + core.astype(F32) + half


def hidden_kernel(lat_ref, own_ref, *refs):
    *cores, half_first, half_rest, hidden_ref, first_ref, last_ref, stats_ref = refs
    sums, squares = 0.0, 0.0
    for frame, edge in enumerate((first_ref, last_ref)):
        cells = slice(frame * PX, (frame + 1) * PX)
        hidden = lat_ref[cells].astype(F32) + three_sums(own_ref, cores, half_first, half_rest, frame)
        hidden_ref[cells] = hidden
        edge[...] = pack(hidden).astype(BF16)
        sums += jnp.sum(hidden, axis=0, keepdims=True)
        squares += jnp.sum(hidden * hidden, axis=0, keepdims=True)
    row = exact_dot(jnp.broadcast_to(sums, (8, LOCAL)), group_to_lane(0))
    row += exact_dot(jnp.broadcast_to(squares, (8, LOCAL)), group_to_lane(LOCAL_GROUPS))
    stats_ref[...] = jnp.broadcast_to(row[0:1], stats_ref.shape)


def hidden_call(lat, shares, size):
    edge = jax.ShapeDtypeStruct((PX // 2, 2 * LOCAL), BF16)
    return pl.pallas_call(
        hidden_kernel,
        out_shape=[
            jax.ShapeDtypeStruct((2 * PX, LOCAL), F32),
            edge,
            edge,
            jax.ShapeDtypeStruct((size, 128), F32),
        ],
        compiler_params=params(),
        cost_estimate=pl.CostEstimate(flops=10 * PX * LOCAL, bytes_accessed=20 * PX * LOCAL, transcendentals=0),
        name="hidden",
    )(lat, *shares)


def blend_kernel(mix_ref, hidden_ref, own_ref, *refs):
    *cores, half_first, half_rest, out_ref = refs
    mix = jnp.full((1, LOCAL), mix_ref[0], F32)
    weight = 1.0 - jax.nn.sigmoid(mix)
    for frame in range(2):
        cells = slice(frame * PX, (frame + 1) * PX)
        branch = three_sums(own_ref, cores, half_first, half_rest, frame).astype(BF16).astype(F32)
        out_ref[cells] = (hidden_ref[cells] + weight * branch).astype(BF16)


def blend_call(mix, hidden, shares):
    whole = pl.BlockSpec(memory_space=pltpu.VMEM)
    return pl.pallas_call(
        blend_kernel,
        in_specs=[pl.BlockSpec(memory_space=pltpu.SMEM)] + [whole] * (4 + CORE_PIECES),
        out_specs=whole,
        out_shape=jax.ShapeDtypeStruct((2 * PX, LOCAL), BF16),
        compiler_params=params(),
        cost_estimate=pl.CostEstimate(flops=6 * PX * LOCAL, bytes_accessed=16 * PX * LOCAL, transcendentals=0),
        name="blend",
    )(mix, hidden, *shares)


def to_core(array, pieces=1):
    rows = array.shape[0] // pieces
    return [lax.ppermute(array[i * rows : (i + 1) * rows], "ch", CORE_SWAP) for i in range(pieces)]


def to_half(array):
    return lax.ppermute(array, "ch", HALF_SWAP)


def settle(array):
    return pl.pallas_call(
        lambda in_ref, out_ref: None,
        in_specs=[pl.BlockSpec(memory_space=pl.ANY)],
        out_specs=pl.BlockSpec(memory_space=pl.ANY),
        out_shape=jax.ShapeDtypeStruct(array.shape, array.dtype),
        input_output_aliases={0: 0},
        compiler_params=pltpu.CompilerParams(vmem_limit_bytes=1024 * 1024),
        cost_estimate=pl.CostEstimate(flops=10**10, bytes_accessed=0, transcendentals=0),
        name="settle",
    )(array)


def reduce_channels(conv, after):
    send, own = conv(after, True)
    first = chip_sum(own, *to_core(send))
    half_first = settle(to_half(first))
    send_rest, own_rest, send, own = conv(first, False)
    half_rest = to_half(chip_sum(own_rest, *to_core(send_rest)))
    return own, *to_core(send, CORE_PIECES), half_first, half_rest


def per_device(latents, spatial_weight, temporal_weight, mix_factor):
    size = lax.axis_size("seq")
    lat = latents.transpose(0, 2, 3, 1).reshape(2 * PX, LOCAL)
    lat_hbm = pltpu.with_memory_space_constraint(lat, pltpu.HBM)
    weight_s = pltpu.with_memory_space_constraint(spatial_weight.reshape(TAPS, WIDE, CH), pltpu.HBM)
    weight_t = temporal_weight.reshape(1, WIDE, CH)
    shares = reduce_channels(functools.partial(spatial_call, lat_hbm, weight_s), lat_hbm)
    hidden, first, last, stats = hidden_call(lat, shares, size)
    next_ = lax.ppermute(first, "seq", [(i + 1, i) for i in range(size - 1)])
    before = lax.ppermute(last, "seq", [(i, i + 1) for i in range(size - 1)])
    stats = lax.all_to_all(stats, "seq", 0, 0, tiled=True)
    shares = reduce_channels(functools.partial(temporal_call, hidden, before, next_, stats, weight_t), hidden)
    out = blend_call(mix_factor, hidden, shares)
    return out.reshape(2, ROWS, COLS, LOCAL).transpose(0, 3, 1, 2)


def solution(mesh):
    placed = (P("seq", "ch", None, None), P(None, None, "ch", None), P(None, "ch", None), P())
    return jax.shard_map(
        per_device,
        mesh=mesh,
        in_specs=placed,
        out_specs=P("seq", "ch", None, None),
        check_vma=False,
    )
```

```python
import functools

import jax
import jax.numpy as jnp
from jax import lax
from jax.experimental import pallas as pl
from jax.experimental.pallas import tpu as pltpu
from jax.sharding import PartitionSpec as P

CH = 1280
GROUPS = 32
GROUP = CH // GROUPS
ROWS = 16
COLS = 32
PX = ROWS * COLS
LOCAL = CH // 4
LOCAL_GROUPS = LOCAL // GROUP
TAPS = 3
WIDE = TAPS * LOCAL
HALF = CH // 2
EPS = 1e-05

CORE_SWAP = [(0, 1), (1, 0), (2, 3), (3, 2)]
HALF_SWAP = [(0, 2), (2, 0), (1, 3), (3, 1)]
FIRST = 256
REST = LOCAL - FIRST
CORE_PIECES = 2
VMEM_LIMIT = 40 * 1024 * 1024
BF16 = jnp.bfloat16
F32 = jnp.float32
HIGHEST = lax.Precision.HIGHEST


def params():
    return pltpu.CompilerParams(vmem_limit_bytes=VMEM_LIMIT)


def silu(v):
    half = 0.5 * v
    return half + half * jnp.tanh(half)


def group_of(channel):
    return (channel * 205) >> 13


def group_block():
    row = lax.broadcasted_iota(jnp.int32, (LOCAL, LOCAL), 0)
    col = lax.broadcasted_iota(jnp.int32, (LOCAL, LOCAL), 1)
    return jnp.where(group_of(row) == group_of(col), 1.0, 0.0)


def group_to_lane(shift):
    row = lax.broadcasted_iota(jnp.int32, (LOCAL, 128), 0)
    lane = lax.broadcasted_iota(jnp.int32, (LOCAL, 128), 1)
    return jnp.where(group_of(row) == lane - shift, 1.0, 0.0)


def lane_to_group(shift):
    lane = lax.broadcasted_iota(jnp.int32, (128, LOCAL), 0)
    col = lax.broadcasted_iota(jnp.int32, (128, LOCAL), 1)
    return jnp.where(group_of(col) == lane - shift, 1.0, 0.0)


def exact_dot(a, b):
    return jnp.dot(a, b, precision=HIGHEST, preferred_element_type=F32)


def pack(block):
    return jnp.concatenate([block[: PX // 2], block[PX // 2 :]], axis=1)


def unpack(ref):
    return jnp.concatenate([ref[:, :LOCAL], ref[:, LOCAL:]], axis=0)


def copy_columns(other, weight_hbm, weight_ref, sems):
    half = lax.axis_index("ch") // 2
    away, home = (1 - half) * HALF, half * HALF
    if other:
        core = lax.axis_index("ch") % 2
        step = HALF - FIRST
        pieces = [(away + core * step, 0, FIRST), (away + (1 - core) * step, FIRST, FIRST)]
    else:
        pieces = [(away + FIRST, 0, 2 * REST), (home, 2 * REST, HALF)]
    copies = []
    for tap in range(weight_hbm.shape[0]):
        copies.append([])
        for i, (start, to, width) in enumerate(pieces):
            source = weight_hbm.at[tap, :, pl.ds(pl.multiple_of(start, 128), width)]
            copy = pltpu.make_async_copy(source, weight_ref.at[tap, :, to : to + width], sems.at[tap, i])
            copy.start()
            copies[-1].append(copy)
    return copies


def store_sums(other, frame, total, outs, total_ref):
    if other:
        send_ref, own_ref = outs
        cells = slice(frame * PX, (frame + 1) * PX)
        own_ref[cells] = total[:, :FIRST].astype(BF16)
        send_ref[cells] = total[:, FIRST:].astype(BF16)
    else:
        total_ref[frame] = total.astype(BF16)
        if frame == 1:
            split_second(total_ref, *outs)


def split_second(total_ref, send_rest, own_rest, send_ref, own_ref):
    core = lax.axis_index("ch") % 2

    def copy(ref, first, width):
        for frame in range(2):
            ref[:, frame * width : (frame + 1) * width] = total_ref[frame, :, first : first + width]

    @pl.when(core == 0)
    def _():
        copy(own_rest, 0, REST)
        copy(send_rest, REST, REST)
        copy(own_ref, 2 * REST, LOCAL)
        copy(send_ref, 2 * REST + LOCAL, LOCAL)

    @pl.when(core == 1)
    def _():
        copy(own_rest, REST, REST)
        copy(send_rest, 0, REST)
        copy(own_ref, 2 * REST + LOCAL, LOCAL)
        copy(send_ref, 2 * REST, LOCAL)


def part_shapes(other):
    if other:
        return [jax.ShapeDtypeStruct((2 * PX, FIRST), BF16)] * 2
    rest, own = jax.ShapeDtypeStruct((PX, 2 * REST), BF16), jax.ShapeDtypeStruct((PX, 2 * LOCAL), BF16)
    return [rest, rest, own, own]


def part_columns(other):
    return 2 * FIRST if other else 2 * REST + HALF


def spatial_taps(lat_ref, taps_ref):
    rows = []
    for frame in range(2):
        lat = lat_ref[frame * PX : (frame + 1) * PX].astype(F32)
        rows.append(jnp.sum(lat, axis=0, keepdims=True))
        rows.append(jnp.sum(lat * lat, axis=0, keepdims=True))
    means = jnp.concatenate(rows + [jnp.zeros((4, LOCAL), F32)], axis=0)
    means = exact_dot(means, group_block()) * (1.0 / (GROUP * PX))
    col = lax.broadcasted_iota(jnp.int32, (COLS, LOCAL), 0)
    def frame_taps(frame):
        mean = means[2 * frame : 2 * frame + 1]
        var = means[2 * frame + 1 : 2 * frame + 2] - mean * mean
        lat = lat_ref[frame * PX : (frame + 1) * PX].astype(F32)
        act = silu((lat - mean) * lax.rsqrt(var + EPS))
        left, right = [], []
        for row in range(ROWS):
            cells = act[row * COLS : (row + 1) * COLS]
            left.append(jnp.where(col == 0, 0.0, pltpu.roll(cells, 1, 0)))
            right.append(jnp.where(col == COLS - 1, 0.0, pltpu.roll(cells, COLS - 1, 0)))
        taps_ref[frame, :COLS] = jnp.zeros((COLS, WIDE), BF16)
        taps_ref[frame, COLS + PX :] = jnp.zeros((COLS, WIDE), BF16)
        inside = slice(COLS, COLS + PX)
        taps_ref[frame, inside, :LOCAL] = jnp.concatenate(left, axis=0).astype(BF16)
        taps_ref[frame, inside, LOCAL : 2 * LOCAL] = act.astype(BF16)
        taps_ref[frame, inside, 2 * LOCAL :] = jnp.concatenate(right, axis=0).astype(BF16)

    return frame_taps


def spatial_kernel(other, lat_hbm, weight_hbm, after_ref, *refs):
    *outs, lat_ref, weight_ref, taps_ref, total_ref, lat_sem, sems = refs
    lat_copy = pltpu.make_async_copy(lat_hbm, lat_ref, lat_sem)
    lat_copy.start()
    copies = copy_columns(other, weight_hbm, weight_ref, sems)
    lat_copy.wait()
    frame_taps = spatial_taps(lat_ref, taps_ref)
    frame_taps(0)
    for copy in sum(copies, []):
        copy.wait()
    for frame in range(2):
        if frame == 0:
            frame_taps(1)
        total = None
        for row_tap in range(TAPS):
            cells = slice(row_tap * COLS, row_tap * COLS + PX)
            term = jnp.dot(taps_ref[frame, cells], weight_ref[row_tap], preferred_element_type=F32)
            total = term if total is None else total + term
        store_sums(other, frame, total, outs, total_ref)


def spatial_call(lat, weight, after, other):
    vmem, anywhere = pl.BlockSpec(memory_space=pltpu.VMEM), pl.BlockSpec(memory_space=pl.ANY)
    shapes, columns = part_shapes(other), part_columns(other)
    return pl.pallas_call(
        functools.partial(spatial_kernel, other),
        in_specs=[anywhere] * 3,
        out_specs=[vmem] * len(shapes),
        out_shape=shapes,
        scratch_shapes=[
            pltpu.VMEM((2 * PX, LOCAL), BF16),
            pltpu.VMEM((TAPS, WIDE, columns), BF16),
            pltpu.VMEM((2, PX + 2 * COLS, WIDE), BF16),
            pltpu.VMEM((2, PX, columns), BF16),
            pltpu.SemaphoreType.DMA,
            pltpu.SemaphoreType.DMA((TAPS, 2)),
        ],
        compiler_params=params(),
        cost_estimate=pl.CostEstimate(
            flops=4 * PX * TAPS * WIDE * columns,
            bytes_accessed=2 * TAPS * WIDE * columns,
            transcendentals=2 * PX * LOCAL,
        ),
        name="spatial",
    )(lat, weight, after)


def temporal_kernel(other, hidden_ref, before_ref, next_ref, stats_ref, weight_hbm, after_ref, *refs):
    *outs, weight_ref, taps_ref, total_ref, sems = refs
    copies = copy_columns(other, weight_hbm, weight_ref, sems)
    seq, size = lax.axis_index("seq"), lax.axis_size("seq")
    sums = jnp.sum(stats_ref[...], axis=0, keepdims=True) * (1.0 / (GROUP * 2 * PX * size))
    sums = jnp.broadcast_to(sums, (8, 128))
    mean = exact_dot(sums, lane_to_group(0))[0:1]
    var = exact_dot(sums, lane_to_group(LOCAL_GROUPS))[0:1] - mean * mean
    scale = lax.rsqrt(var + EPS)

    def act(values):
        return silu((values - mean) * scale)

    def put(values, *places):
        values = values.astype(BF16)
        for frame, tap in places:
            taps_ref[frame, :, tap * LOCAL : (tap + 1) * LOCAL] = values

    put(act(unpack(before_ref).astype(F32)) * jnp.where(seq == 0, 0.0, 1.0), (0, 0))
    put(act(hidden_ref[:PX]), (0, 1), (1, 0))
    put(act(hidden_ref[PX:]), (0, 2), (1, 1))
    for copy in copies[0]:
        copy.wait()
    put(act(unpack(next_ref).astype(F32)) * jnp.where(seq == size - 1, 0.0, 1.0), (1, 2))
    for frame in range(2):
        total = jnp.dot(taps_ref[frame], weight_ref[0], preferred_element_type=F32)
        store_sums(other, frame, total, outs, total_ref)


def temporal_call(hidden, before, next_, stats, weight, after, other):
    vmem = pl.BlockSpec(memory_space=pltpu.VMEM)
    shapes, columns = part_shapes(other), part_columns(other)
    return pl.pallas_call(
        functools.partial(temporal_kernel, other),
        in_specs=[vmem] * 4 + [pl.BlockSpec(memory_space=pl.ANY)] * 2,
        out_specs=[vmem] * len(shapes),
        out_shape=shapes,
        scratch_shapes=[
            pltpu.VMEM((1, WIDE, columns), BF16),
            pltpu.VMEM((2, PX, WIDE), BF16),
            pltpu.VMEM((2, PX, columns), BF16),
            pltpu.SemaphoreType.DMA((1, 2)),
        ],
        compiler_params=params(),
        cost_estimate=pl.CostEstimate(
            flops=4 * PX * WIDE * columns,
            bytes_accessed=2 * WIDE * columns,
            transcendentals=4 * PX * LOCAL,
        ),
        name="temporal",
    )(hidden, before, next_, stats, weight, after)


def chip_sum_kernel(own_ref, got_ref, out_ref):
    out_ref[...] = (own_ref[...].astype(F32) + got_ref[...].astype(F32)).astype(BF16)


def chip_sum(own, got):
    return pl.pallas_call(
        chip_sum_kernel,
        out_shape=jax.ShapeDtypeStruct(own.shape, BF16),
        compiler_params=pltpu.CompilerParams(vmem_limit_bytes=8 * 1024 * 1024),
        cost_estimate=pl.CostEstimate(flops=4 * 10**9, bytes_accessed=6 * own.size, transcendentals=0),
        name="chip_sum",
    )(own, got)


def chip_part(own_ref, core_refs, frame):
    cols = slice(frame * LOCAL, (frame + 1) * LOCAL)
    core = jnp.concatenate([ref[:, cols] for ref in core_refs], axis=0)
    return own_ref[:, cols].astype(F32) + core.astype(F32)


def half_part(first_ref, rest_ref, frame):
    first = first_ref[frame * PX : (frame + 1) * PX].astype(F32)
    rest = rest_ref[:, frame * REST : (frame + 1) * REST].astype(F32)
    return jnp.where(
        lax.axis_index("ch") % 2 == 0,
        jnp.concatenate([first, rest], axis=1),
        jnp.concatenate([rest, first], axis=1),
    )


def small_cost():
    return pl.CostEstimate(flops=10 * PX * LOCAL, bytes_accessed=20 * PX * LOCAL, transcendentals=0)


def base_kernel(lat_ref, own_ref, *refs):
    *cores, base_ref = refs
    for frame in range(2):
        cells = slice(frame * PX, (frame + 1) * PX)
        base_ref[cells] = lat_ref[cells].astype(F32) + chip_part(own_ref, cores, frame)


def base_call(lat, own, cores):
    return pl.pallas_call(
        base_kernel,
        out_shape=jax.ShapeDtypeStruct((2 * PX, LOCAL), F32),
        compiler_params=params(),
        cost_estimate=small_cost(),
        name="base",
    )(lat, own, *cores)


def hidden_kernel(base_ref, half_first, half_rest, hidden_ref, first_ref, last_ref, stats_ref):
    sums, squares = 0.0, 0.0
    for frame, edge in enumerate((first_ref, last_ref)):
        cells = slice(frame * PX, (frame + 1) * PX)
        hidden = base_ref[cells] + half_part(half_first, half_rest, frame)
        hidden_ref[cells] = hidden
        edge[...] = pack(hidden).astype(BF16)
        sums += jnp.sum(hidden, axis=0, keepdims=True)
        squares += jnp.sum(hidden * hidden, axis=0, keepdims=True)
    row = exact_dot(jnp.broadcast_to(sums, (8, LOCAL)), group_to_lane(0))
    row += exact_dot(jnp.broadcast_to(squares, (8, LOCAL)), group_to_lane(LOCAL_GROUPS))
    stats_ref[...] = jnp.broadcast_to(row[0:1], stats_ref.shape)


def hidden_call(base, half_first, half_rest, size):
    edge = jax.ShapeDtypeStruct((PX // 2, 2 * LOCAL), BF16)
    return pl.pallas_call(
        hidden_kernel,
        out_shape=[
            jax.ShapeDtypeStruct((2 * PX, LOCAL), F32),
            edge,
            edge,
            jax.ShapeDtypeStruct((size, 128), F32),
        ],
        compiler_params=params(),
        cost_estimate=small_cost(),
        name="hidden",
    )(base, half_first, half_rest)


def branch_weight(mix_ref):
    return 1.0 - jax.nn.sigmoid(jnp.full((1, LOCAL), mix_ref[0], F32))


def mixed_kernel(mix_ref, hidden_ref, own_ref, *refs):
    *cores, mixed_ref = refs
    for frame in range(2):
        cells = slice(frame * PX, (frame + 1) * PX)
        mixed_ref[cells] = hidden_ref[cells] + branch_weight(mix_ref) * chip_part(own_ref, cores, frame)


def blend_kernel(mix_ref, mixed_ref, half_first, half_rest, out_hbm, out_ref, sems):
    copies = []
    for frame in range(2):
        cells = slice(frame * PX, (frame + 1) * PX)
        half = half_part(half_first, half_rest, frame)
        out_ref[cells] = (mixed_ref[cells] + branch_weight(mix_ref) * half).astype(BF16)
        copies.append(pltpu.make_async_copy(out_ref.at[cells], out_hbm.at[cells], sems.at[frame]))
        copies[-1].start()
    for copy in copies:
        copy.wait()


def blend_call(mix, *arrays):
    whole = pl.BlockSpec(memory_space=pltpu.VMEM)
    return pl.pallas_call(
        blend_kernel,
        in_specs=[pl.BlockSpec(memory_space=pltpu.SMEM)] + [whole] * len(arrays),
        out_specs=pl.BlockSpec(memory_space=pl.ANY),
        out_shape=jax.ShapeDtypeStruct((2 * PX, LOCAL), BF16),
        scratch_shapes=[pltpu.VMEM((2 * PX, LOCAL), BF16), pltpu.SemaphoreType.DMA((2,))],
        compiler_params=params(),
        cost_estimate=small_cost(),
        name="blend",
    )(mix, *arrays)


def mix_call(kernel, mix, dtype, name, *arrays):
    whole = pl.BlockSpec(memory_space=pltpu.VMEM)
    return pl.pallas_call(
        kernel,
        in_specs=[pl.BlockSpec(memory_space=pltpu.SMEM)] + [whole] * len(arrays),
        out_specs=whole,
        out_shape=jax.ShapeDtypeStruct((2 * PX, LOCAL), dtype),
        compiler_params=params(),
        cost_estimate=small_cost(),
        name=name,
    )(mix, *arrays)


def to_core(array, pieces=1):
    rows = array.shape[0] // pieces
    return [lax.ppermute(array[i * rows : (i + 1) * rows], "ch", CORE_SWAP) for i in range(pieces)]


def to_half(array):
    return lax.ppermute(array, "ch", HALF_SWAP)


def settle(array, after):
    anywhere = pl.BlockSpec(memory_space=pl.ANY)
    return pl.pallas_call(
        lambda in_ref, after_ref, out_ref: None,
        in_specs=[anywhere, anywhere],
        out_specs=anywhere,
        out_shape=jax.ShapeDtypeStruct(array.shape, array.dtype),
        input_output_aliases={0: 0},
        compiler_params=pltpu.CompilerParams(vmem_limit_bytes=1024 * 1024),
        cost_estimate=pl.CostEstimate(flops=10**10, bytes_accessed=0, transcendentals=0),
        name="settle",
    )(array, after)


def reduce_channels(first, second, combine):
    send, own = first()
    chip = chip_sum(own, *to_core(send))
    half_first = to_half(chip)
    send_rest, own_rest, send, own = second(chip)
    half_rest = to_half(chip_sum(own_rest, *to_core(send_rest)))
    combined = combine(own, to_core(send, CORE_PIECES))
    return combined, settle(half_first, combined), half_rest


def per_device(latents, spatial_weight, temporal_weight, mix_factor):
    size = lax.axis_size("seq")
    lat = latents.transpose(0, 2, 3, 1).reshape(2 * PX, LOCAL)
    lat_hbm = pltpu.with_memory_space_constraint(lat, pltpu.HBM)
    weight_s = pltpu.with_memory_space_constraint(spatial_weight.reshape(TAPS, WIDE, CH), pltpu.HBM)
    weight_t = temporal_weight.reshape(1, WIDE, CH)
    base, half_first, half_rest = reduce_channels(
        lambda: spatial_call(lat_hbm, weight_s, lat_hbm, True),
        lambda after: spatial_call(lat_hbm, weight_s, after, False),
        lambda own, cores: base_call(lat, own, cores),
    )
    hidden, first, last, stats = hidden_call(base, half_first, half_rest, size)
    next_ = lax.ppermute(first, "seq", [(i + 1, i) for i in range(size - 1)])
    before = lax.ppermute(last, "seq", [(i, i + 1) for i in range(size - 1)])
    stats = lax.all_to_all(stats, "seq", 0, 0, tiled=True)
    mixed, half_first, half_rest = reduce_channels(
        lambda: temporal_call(hidden, before, next_, stats, weight_t, hidden, True),
        lambda after: temporal_call(hidden, before, next_, stats, weight_t, after, False),
        lambda own, cores: mix_call(mixed_kernel, mix_factor, F32, "mixed", hidden, own, *cores),
    )
    out = blend_call(mix_factor, mixed, half_first, half_rest)
    return out.reshape(2, ROWS, COLS, LOCAL).transpose(0, 3, 1, 2)


def solution(mesh):
    placed = (P("seq", "ch", None, None), P(None, None, "ch", None), P(None, "ch", None), P())
    return jax.shard_map(
        per_device,
        mesh=mesh,
        in_specs=placed,
        out_specs=P("seq", "ch", None, None),
        check_vma=False,
    )
```

```python
import functools

import jax
import jax.numpy as jnp
from jax import lax
from jax.experimental import pallas as pl
from jax.experimental.pallas import tpu as pltpu
from jax.sharding import PartitionSpec as P

CH = 1280
GROUPS = 32
GROUP = CH // GROUPS
ROWS = 16
COLS = 32
PX = ROWS * COLS
LOCAL = CH // 4
LOCAL_GROUPS = LOCAL // GROUP
TAPS = 3
WIDE = TAPS * LOCAL
HALF = CH // 2
EPS = 1e-05

CORE_SWAP = [(0, 1), (1, 0), (2, 3), (3, 2)]
HALF_SWAP = [(0, 2), (2, 0), (1, 3), (3, 1)]
FIRST = 256
REST = LOCAL - FIRST
CORE_PIECES = 2
VMEM_LIMIT = 40 * 1024 * 1024
BF16 = jnp.bfloat16
F32 = jnp.float32
HIGHEST = lax.Precision.HIGHEST


def params():
    return pltpu.CompilerParams(vmem_limit_bytes=VMEM_LIMIT)


def silu(v):
    half = 0.5 * v
    return half + half * jnp.tanh(half)


def group_of(channel):
    return (channel * 205) >> 13


def group_block():
    row = lax.broadcasted_iota(jnp.int32, (LOCAL, LOCAL), 0)
    col = lax.broadcasted_iota(jnp.int32, (LOCAL, LOCAL), 1)
    return jnp.where(group_of(row) == group_of(col), 1.0, 0.0)


def group_to_lane():
    row = lax.broadcasted_iota(jnp.int32, (LOCAL, 128), 0)
    lane = lax.broadcasted_iota(jnp.int32, (LOCAL, 128), 1)
    return jnp.where(group_of(row) == lane, 1.0, 0.0)


def lane_to_group():
    lane = lax.broadcasted_iota(jnp.int32, (128, LOCAL), 0)
    col = lax.broadcasted_iota(jnp.int32, (128, LOCAL), 1)
    return jnp.where(group_of(col) == lane, 1.0, 0.0)


def exact_dot(a, b):
    return jnp.dot(a, b, precision=HIGHEST, preferred_element_type=F32)


def pack(block):
    return jnp.concatenate([block[: PX // 2], block[PX // 2 :]], axis=1)


def unpack(ref):
    return jnp.concatenate([ref[:, :LOCAL], ref[:, LOCAL:]], axis=0)


def copy_columns(other, weight_hbm, weight_ref, sems):
    half = lax.axis_index("ch") // 2
    away, home = (1 - half) * HALF, half * HALF
    if other:
        core = lax.axis_index("ch") % 2
        step = HALF - FIRST
        pieces = [(away + core * step, 0, FIRST), (away + (1 - core) * step, FIRST, FIRST)]
    else:
        pieces = [(away + FIRST, 0, 2 * REST), (home, 2 * REST, HALF)]
    copies = []
    for tap in range(weight_hbm.shape[0]):
        copies.append([])
        for i, (start, to, width) in enumerate(pieces):
            source = weight_hbm.at[tap, :, pl.ds(pl.multiple_of(start, 128), width)]
            copy = pltpu.make_async_copy(source, weight_ref.at[tap, :, to : to + width], sems.at[tap, i])
            copy.start()
            copies[-1].append(copy)
    return copies


def store_sums(other, frame, total, outs, total_ref):
    if other:
        send_ref, own_ref = outs
        cells = slice(frame * PX, (frame + 1) * PX)
        own_ref[cells] = total[:, :FIRST].astype(BF16)
        send_ref[cells] = total[:, FIRST:].astype(BF16)
    else:
        total_ref[frame] = total.astype(BF16)
        if frame == 1:
            split_second(total_ref, *outs)


def split_second(total_ref, send_rest, own_rest, send_ref, own_ref):
    core = lax.axis_index("ch") % 2

    def copy(ref, first, width):
        for frame in range(2):
            ref[:, frame * width : (frame + 1) * width] = total_ref[frame, :, first : first + width]

    @pl.when(core == 0)
    def _():
        copy(own_rest, 0, REST)
        copy(send_rest, REST, REST)
        copy(own_ref, 2 * REST, LOCAL)
        copy(send_ref, 2 * REST + LOCAL, LOCAL)

    @pl.when(core == 1)
    def _():
        copy(own_rest, REST, REST)
        copy(send_rest, 0, REST)
        copy(own_ref, 2 * REST + LOCAL, LOCAL)
        copy(send_ref, 2 * REST, LOCAL)


def part_shapes(other):
    if other:
        return [jax.ShapeDtypeStruct((2 * PX, FIRST), BF16)] * 2
    rest, own = jax.ShapeDtypeStruct((PX, 2 * REST), BF16), jax.ShapeDtypeStruct((PX, 2 * LOCAL), BF16)
    return [rest, rest, own, own]


def part_columns(other):
    return 2 * FIRST if other else 2 * REST + HALF


def spatial_taps(lat_ref, taps_ref):
    rows = []
    for frame in range(2):
        lat = lat_ref[frame * PX : (frame + 1) * PX].astype(F32)
        rows.append(jnp.sum(lat, axis=0, keepdims=True))
        rows.append(jnp.sum(lat * lat, axis=0, keepdims=True))
    means = jnp.concatenate(rows + [jnp.zeros((4, LOCAL), F32)], axis=0)
    means = exact_dot(means, group_block()) * (1.0 / (GROUP * PX))
    col = lax.broadcasted_iota(jnp.int32, (COLS, LOCAL), 0)
    def frame_taps(frame):
        mean = means[2 * frame : 2 * frame + 1]
        var = means[2 * frame + 1 : 2 * frame + 2] - mean * mean
        lat = lat_ref[frame * PX : (frame + 1) * PX].astype(F32)
        act = silu((lat - mean) * lax.rsqrt(var + EPS))
        left, right = [], []
        for row in range(ROWS):
            cells = act[row * COLS : (row + 1) * COLS]
            left.append(jnp.where(col == 0, 0.0, pltpu.roll(cells, 1, 0)))
            right.append(jnp.where(col == COLS - 1, 0.0, pltpu.roll(cells, COLS - 1, 0)))
        taps_ref[frame, :COLS] = jnp.zeros((COLS, WIDE), BF16)
        taps_ref[frame, COLS + PX :] = jnp.zeros((COLS, WIDE), BF16)
        inside = slice(COLS, COLS + PX)
        taps_ref[frame, inside, :LOCAL] = jnp.concatenate(left, axis=0).astype(BF16)
        taps_ref[frame, inside, LOCAL : 2 * LOCAL] = act.astype(BF16)
        taps_ref[frame, inside, 2 * LOCAL :] = jnp.concatenate(right, axis=0).astype(BF16)

    return frame_taps


def spatial_kernel(other, lat_hbm, weight_hbm, after_ref, *refs):
    *outs, lat_ref, weight_ref, taps_ref, total_ref, lat_sem, sems = refs
    lat_copy = pltpu.make_async_copy(lat_hbm, lat_ref, lat_sem)
    lat_copy.start()
    copies = copy_columns(other, weight_hbm, weight_ref, sems)
    lat_copy.wait()
    frame_taps = spatial_taps(lat_ref, taps_ref)
    frame_taps(0)
    for copy in sum(copies, []):
        copy.wait()
    for frame in range(2):
        if frame == 0:
            frame_taps(1)
        total = None
        for row_tap in range(TAPS):
            cells = slice(row_tap * COLS, row_tap * COLS + PX)
            term = jnp.dot(taps_ref[frame, cells], weight_ref[row_tap], preferred_element_type=F32)
            total = term if total is None else total + term
        store_sums(other, frame, total, outs, total_ref)


def spatial_call(lat, weight, after, other):
    vmem, anywhere = pl.BlockSpec(memory_space=pltpu.VMEM), pl.BlockSpec(memory_space=pl.ANY)
    shapes, columns = part_shapes(other), part_columns(other)
    return pl.pallas_call(
        functools.partial(spatial_kernel, other),
        in_specs=[anywhere] * 3,
        out_specs=[vmem] * len(shapes),
        out_shape=shapes,
        scratch_shapes=[
            pltpu.VMEM((2 * PX, LOCAL), BF16),
            pltpu.VMEM((TAPS, WIDE, columns), BF16),
            pltpu.VMEM((2, PX + 2 * COLS, WIDE), BF16),
            pltpu.VMEM((2, PX, columns), BF16),
            pltpu.SemaphoreType.DMA,
            pltpu.SemaphoreType.DMA((TAPS, 2)),
        ],
        compiler_params=params(),
        cost_estimate=pl.CostEstimate(
            flops=4 * PX * TAPS * WIDE * columns,
            bytes_accessed=2 * TAPS * WIDE * columns,
            transcendentals=2 * PX * LOCAL,
        ),
        name="spatial",
    )(lat, weight, after)


def temporal_kernel(other, hidden_ref, across_ref, pair_ref, stats_ref, weight_hbm, after_ref, *refs):
    *outs, weight_ref, taps_ref, total_ref, sems = refs
    copies = copy_columns(other, weight_hbm, weight_ref, sems)
    seq, size = lax.axis_index("seq"), lax.axis_size("seq")
    sums = jnp.sum(stats_ref[...], axis=0, keepdims=True) * (1.0 / (GROUP * 2 * PX * size))
    squares = pltpu.roll(jnp.broadcast_to(sums, (8, 128)), 128 - LOCAL_GROUPS, 1)[0:1]
    both = exact_dot(jnp.concatenate([sums, squares, jnp.zeros((6, 128), F32)], axis=0), lane_to_group())
    mean = both[0:1]
    var = both[1:2] - mean * mean
    scale = lax.rsqrt(var + EPS)

    def act(values):
        return silu((values - mean) * scale)

    def put(values, *places):
        values = values.astype(BF16)
        for frame, tap in places:
            taps_ref[frame, :, tap * LOCAL : (tap + 1) * LOCAL] = values

    def halo(even_ref, odd_ref, edge):
        values = jnp.where(seq % 2 == 0, unpack(even_ref), unpack(odd_ref))
        return act(values.astype(F32)) * jnp.where(edge, 0.0, 1.0)

    put(halo(across_ref, pair_ref, seq == 0), (0, 0))
    put(act(hidden_ref[:PX]), (0, 1), (1, 0))
    put(act(hidden_ref[PX:]), (0, 2), (1, 1))
    for copy in copies[0]:
        copy.wait()
    put(halo(pair_ref, across_ref, seq == size - 1), (1, 2))
    for frame in range(2):
        total = jnp.dot(taps_ref[frame], weight_ref[0], preferred_element_type=F32)
        store_sums(other, frame, total, outs, total_ref)


def temporal_call(hidden, halos, stats, weight, after, other):
    vmem = pl.BlockSpec(memory_space=pltpu.VMEM)
    shapes, columns = part_shapes(other), part_columns(other)
    return pl.pallas_call(
        functools.partial(temporal_kernel, other),
        in_specs=[vmem] * 4 + [pl.BlockSpec(memory_space=pl.ANY)] * 2,
        out_specs=[vmem] * len(shapes),
        out_shape=shapes,
        scratch_shapes=[
            pltpu.VMEM((1, WIDE, columns), BF16),
            pltpu.VMEM((2, PX, WIDE), BF16),
            pltpu.VMEM((2, PX, columns), BF16),
            pltpu.SemaphoreType.DMA((1, 2)),
        ],
        compiler_params=params(),
        cost_estimate=pl.CostEstimate(
            flops=4 * PX * WIDE * columns,
            bytes_accessed=2 * WIDE * columns,
            transcendentals=4 * PX * LOCAL,
        ),
        name="temporal",
    )(hidden, *halos[::-1], stats, weight, after)


def chip_sum_kernel(own_ref, got_ref, out_ref):
    out_ref[...] = (own_ref[...].astype(F32) + got_ref[...].astype(F32)).astype(BF16)


def chip_sum(own, got):
    return pl.pallas_call(
        chip_sum_kernel,
        out_shape=jax.ShapeDtypeStruct(own.shape, BF16),
        compiler_params=pltpu.CompilerParams(vmem_limit_bytes=8 * 1024 * 1024),
        cost_estimate=pl.CostEstimate(flops=4 * 10**9, bytes_accessed=6 * own.size, transcendentals=0),
        name="chip_sum",
    )(own, got)


def chip_part(own_ref, core_refs, frame):
    cols = slice(frame * LOCAL, (frame + 1) * LOCAL)
    core = jnp.concatenate([ref[:, cols] for ref in core_refs], axis=0)
    return own_ref[:, cols].astype(F32) + core.astype(F32)


def half_part(first_ref, rest_ref, frame):
    first = first_ref[frame * PX : (frame + 1) * PX].astype(F32)
    rest = rest_ref[:, frame * REST : (frame + 1) * REST].astype(F32)
    return jnp.where(
        lax.axis_index("ch") % 2 == 0,
        jnp.concatenate([first, rest], axis=1),
        jnp.concatenate([rest, first], axis=1),
    )


def small_cost():
    return pl.CostEstimate(flops=10 * PX * LOCAL, bytes_accessed=20 * PX * LOCAL, transcendentals=0)


def base_kernel(lat_ref, own_ref, *refs):
    *cores, base_ref = refs
    for frame in range(2):
        cells = slice(frame * PX, (frame + 1) * PX)
        base_ref[cells] = lat_ref[cells].astype(F32) + chip_part(own_ref, cores, frame)


def base_call(lat, own, cores):
    return pl.pallas_call(
        base_kernel,
        out_shape=jax.ShapeDtypeStruct((2 * PX, LOCAL), F32),
        compiler_params=params(),
        cost_estimate=small_cost(),
        name="base",
    )(lat, own, *cores)


def hidden_kernel(base_ref, half_first, half_rest, hidden_ref, edges_ref, stats_ref):
    odd = lax.axis_index("seq") % 2
    sums, squares = 0.0, 0.0
    for frame in range(2):
        cells = slice(frame * PX, (frame + 1) * PX)
        hidden = base_ref[cells] + half_part(half_first, half_rest, frame)
        hidden_ref[cells] = hidden
        slot = 1 - odd if frame == 0 else odd
        edges_ref[pl.ds(pl.multiple_of(slot * (PX // 2), PX // 2), PX // 2)] = pack(hidden).astype(BF16)
        sums += jnp.sum(hidden, axis=0, keepdims=True)
        squares += jnp.sum(hidden * hidden, axis=0, keepdims=True)
    both = jnp.concatenate([sums, squares, jnp.zeros((6, LOCAL), F32)], axis=0)
    both = exact_dot(both, group_to_lane())
    row = both[0:1] + pltpu.roll(both, LOCAL_GROUPS, 1)[1:2]
    stats_ref[...] = jnp.broadcast_to(row, stats_ref.shape)


def hidden_call(base, half_first, half_rest, size):
    return pl.pallas_call(
        hidden_kernel,
        out_shape=[
            jax.ShapeDtypeStruct((2 * PX, LOCAL), F32),
            jax.ShapeDtypeStruct((PX, 2 * LOCAL), BF16),
            jax.ShapeDtypeStruct((size, 128), F32),
        ],
        compiler_params=params(),
        cost_estimate=small_cost(),
        name="hidden",
    )(base, half_first, half_rest)


def branch_weight(mix_ref):
    return 1.0 - jax.nn.sigmoid(jnp.full((1, LOCAL), mix_ref[0], F32))


def mixed_kernel(mix_ref, hidden_ref, own_ref, *refs):
    *cores, mixed_ref = refs
    for frame in range(2):
        cells = slice(frame * PX, (frame + 1) * PX)
        mixed_ref[cells] = hidden_ref[cells] + branch_weight(mix_ref) * chip_part(own_ref, cores, frame)


def blend_kernel(mix_ref, mixed_ref, half_first, half_rest, out_hbm, out_ref, sems):
    copies = []
    for frame in range(2):
        cells = slice(frame * PX, (frame + 1) * PX)
        half = half_part(half_first, half_rest, frame)
        out_ref[cells] = (mixed_ref[cells] + branch_weight(mix_ref) * half).astype(BF16)
        copies.append(pltpu.make_async_copy(out_ref.at[cells], out_hbm.at[cells], sems.at[frame]))
        copies[-1].start()
    for copy in copies:
        copy.wait()


def blend_call(mix, *arrays):
    whole = pl.BlockSpec(memory_space=pltpu.VMEM)
    return pl.pallas_call(
        blend_kernel,
        in_specs=[pl.BlockSpec(memory_space=pltpu.SMEM)] + [whole] * len(arrays),
        out_specs=pl.BlockSpec(memory_space=pl.ANY),
        out_shape=jax.ShapeDtypeStruct((2 * PX, LOCAL), BF16),
        scratch_shapes=[pltpu.VMEM((2 * PX, LOCAL), BF16), pltpu.SemaphoreType.DMA((2,))],
        compiler_params=params(),
        cost_estimate=small_cost(),
        name="blend",
    )(mix, *arrays)


def mix_call(kernel, mix, dtype, name, *arrays):
    whole = pl.BlockSpec(memory_space=pltpu.VMEM)
    return pl.pallas_call(
        kernel,
        in_specs=[pl.BlockSpec(memory_space=pltpu.SMEM)] + [whole] * len(arrays),
        out_specs=whole,
        out_shape=jax.ShapeDtypeStruct((2 * PX, LOCAL), dtype),
        compiler_params=params(),
        cost_estimate=small_cost(),
        name=name,
    )(mix, *arrays)


def to_core(array, pieces=1):
    rows = array.shape[0] // pieces
    return [lax.ppermute(array[i * rows : (i + 1) * rows], "ch", CORE_SWAP) for i in range(pieces)]


def to_half(array):
    return lax.ppermute(array, "ch", HALF_SWAP)


def settle(array, after):
    anywhere = pl.BlockSpec(memory_space=pl.ANY)
    return pl.pallas_call(
        lambda in_ref, after_ref, out_ref: None,
        in_specs=[anywhere, anywhere],
        out_specs=anywhere,
        out_shape=jax.ShapeDtypeStruct(array.shape, array.dtype),
        input_output_aliases={0: 0},
        compiler_params=pltpu.CompilerParams(vmem_limit_bytes=1024 * 1024),
        cost_estimate=pl.CostEstimate(flops=10**10, bytes_accessed=0, transcendentals=0),
        name="settle",
    )(array, after)


def reduce_channels(first, second, combine):
    send, own = first()
    chip = chip_sum(own, *to_core(send))
    half_first = to_half(chip)
    send_rest, own_rest, send, own = second(chip)
    half_rest = to_half(chip_sum(own_rest, *to_core(send_rest)))
    combined = combine(own, to_core(send, CORE_PIECES))
    return combined, settle(half_first, combined), half_rest


def per_device(latents, spatial_weight, temporal_weight, mix_factor):
    size = lax.axis_size("seq")
    lat = latents.transpose(0, 2, 3, 1).reshape(2 * PX, LOCAL)
    lat_hbm = pltpu.with_memory_space_constraint(lat, pltpu.HBM)
    weight_s = pltpu.with_memory_space_constraint(spatial_weight.reshape(TAPS, WIDE, CH), pltpu.HBM)
    weight_t = temporal_weight.reshape(1, WIDE, CH)
    base, half_first, half_rest = reduce_channels(
        lambda: spatial_call(lat_hbm, weight_s, lat_hbm, True),
        lambda after: spatial_call(lat_hbm, weight_s, after, False),
        lambda own, cores: base_call(lat, own, cores),
    )
    hidden, edges, stats = hidden_call(base, half_first, half_rest, size)
    halos = []
    for start in range(2):
        pairs = [(i, i + 1) for i in range(start, size - 1, 2)]
        edge = edges[start * (PX // 2) : (start + 1) * (PX // 2)]
        halos.append(lax.ppermute(edge, "seq", pairs + [(b, a) for a, b in pairs]))
    stats = lax.all_to_all(stats, "seq", 0, 0, tiled=True)
    mixed, half_first, half_rest = reduce_channels(
        lambda: temporal_call(hidden, halos, stats, weight_t, hidden, True),
        lambda after: temporal_call(hidden, halos, stats, weight_t, after, False),
        lambda own, cores: mix_call(mixed_kernel, mix_factor, F32, "mixed", hidden, own, *cores),
    )
    out = blend_call(mix_factor, mixed, half_first, half_rest)
    return out.reshape(2, ROWS, COLS, LOCAL).transpose(0, 3, 1, 2)


def solution(mesh):
    placed = (P("seq", "ch", None, None), P(None, None, "ch", None), P(None, "ch", None), P())
    return jax.shard_map(
        per_device,
        mesh=mesh,
        in_specs=placed,
        out_specs=P("seq", "ch", None, None),
        check_vma=False,
    )
```

```python
import functools

import jax
import jax.numpy as jnp
from jax import lax
from jax.experimental import pallas as pl
from jax.experimental.pallas import tpu as pltpu
from jax.sharding import PartitionSpec as P

CH = 1280
GROUPS = 32
GROUP = CH // GROUPS
ROWS = 16
COLS = 32
PX = ROWS * COLS
LOCAL = CH // 4
LOCAL_GROUPS = LOCAL // GROUP
TAPS = 3
WIDE = TAPS * LOCAL
HALF = CH // 2
EPS = 1e-05

CORE_SWAP = [(0, 1), (1, 0), (2, 3), (3, 2)]
HALF_SWAP = [(0, 2), (2, 0), (1, 3), (3, 1)]
FIRST = 256
REST = LOCAL - FIRST
CORE_PIECES = 2
VMEM_LIMIT = 40 * 1024 * 1024
BF16 = jnp.bfloat16
F32 = jnp.float32
HIGHEST = lax.Precision.HIGHEST


def params():
    return pltpu.CompilerParams(vmem_limit_bytes=VMEM_LIMIT)


def silu(v):
    half = 0.5 * v
    return half + half * jnp.tanh(half)


def group_of(channel):
    return (channel * 205) >> 13


def group_block():
    row = lax.broadcasted_iota(jnp.int32, (LOCAL, LOCAL), 0)
    col = lax.broadcasted_iota(jnp.int32, (LOCAL, LOCAL), 1)
    return jnp.where(group_of(row) == group_of(col), 1.0, 0.0)


def group_to_lane():
    row = lax.broadcasted_iota(jnp.int32, (LOCAL, 128), 0)
    lane = lax.broadcasted_iota(jnp.int32, (LOCAL, 128), 1)
    return jnp.where(group_of(row) == lane, 1.0, 0.0)


def lane_to_group():
    lane = lax.broadcasted_iota(jnp.int32, (128, LOCAL), 0)
    col = lax.broadcasted_iota(jnp.int32, (128, LOCAL), 1)
    return jnp.where(group_of(col) == lane, 1.0, 0.0)


def exact_dot(a, b):
    return jnp.dot(a, b, precision=HIGHEST, preferred_element_type=F32)


def pack(block):
    return jnp.concatenate([block[: PX // 2], block[PX // 2 :]], axis=1)


def unpack(ref):
    return jnp.concatenate([ref[:, :LOCAL], ref[:, LOCAL:]], axis=0)


def start_copies(pieces, weight_hbm, weight_ref, sems):
    copies = []
    for tap in range(weight_hbm.shape[0]):
        for i, (start, to, width) in enumerate(pieces):
            source = weight_hbm.at[tap, :, pl.ds(pl.multiple_of(start, 128), width)]
            copy = pltpu.make_async_copy(source, weight_ref.at[tap, :, to : to + width], sems.at[tap, i])
            copy.start()
            copies.append(copy)
    return copies


def first_columns(own):
    index = lax.axis_index("ch")
    half, core = index // 2, index % 2
    core = core if own else 1 - core
    return (1 - half) * HALF + core * (HALF - FIRST)


def copy_columns(other, weight_hbm, weight_ref, sems):
    if other:
        pieces = [(first_columns(True), 0, FIRST), (first_columns(False), FIRST, FIRST)]
    else:
        half = lax.axis_index("ch") // 2
        pieces = [((1 - half) * HALF + FIRST, 0, 2 * REST), (half * HALF, 2 * REST, HALF)]
    return start_copies(pieces, weight_hbm, weight_ref, sems)


def store_sums(other, frame, total, outs, total_ref):
    if other:
        send_ref, own_ref = outs
        cells = slice(frame * PX, (frame + 1) * PX)
        own_ref[cells] = total[:, :FIRST].astype(BF16)
        send_ref[cells] = total[:, FIRST:].astype(BF16)
    else:
        total_ref[frame] = total.astype(BF16)
        if frame == 1:
            split_second(total_ref, *outs)


def split_second(total_ref, send_rest, own_rest, send_ref, own_ref):
    core = lax.axis_index("ch") % 2

    def copy(ref, first, width):
        for frame in range(2):
            ref[:, frame * width : (frame + 1) * width] = total_ref[frame, :, first : first + width]

    @pl.when(core == 0)
    def _():
        copy(own_rest, 0, REST)
        copy(send_rest, REST, REST)
        copy(own_ref, 2 * REST, LOCAL)
        copy(send_ref, 2 * REST + LOCAL, LOCAL)

    @pl.when(core == 1)
    def _():
        copy(own_rest, REST, REST)
        copy(send_rest, 0, REST)
        copy(own_ref, 2 * REST + LOCAL, LOCAL)
        copy(send_ref, 2 * REST, LOCAL)


def part_shapes(other):
    if other:
        return [jax.ShapeDtypeStruct((2 * PX, FIRST), BF16)] * 2
    rest, own = jax.ShapeDtypeStruct((PX, 2 * REST), BF16), jax.ShapeDtypeStruct((PX, 2 * LOCAL), BF16)
    return [rest, rest, own, own]


def part_columns(other):
    return 2 * FIRST if other else 2 * REST + HALF


def spatial_taps(lat_ref, taps_ref):
    rows = []
    for frame in range(2):
        lat = lat_ref[frame * PX : (frame + 1) * PX].astype(F32)
        rows.append(jnp.sum(lat, axis=0, keepdims=True))
        rows.append(jnp.sum(lat * lat, axis=0, keepdims=True))
    means = jnp.concatenate(rows + [jnp.zeros((4, LOCAL), F32)], axis=0)
    means = exact_dot(means, group_block()) * (1.0 / (GROUP * PX))
    col = lax.broadcasted_iota(jnp.int32, (COLS, LOCAL), 0)
    def frame_taps(frame):
        mean = means[2 * frame : 2 * frame + 1]
        var = means[2 * frame + 1 : 2 * frame + 2] - mean * mean
        lat = lat_ref[frame * PX : (frame + 1) * PX].astype(F32)
        act = silu((lat - mean) * lax.rsqrt(var + EPS))
        left, right = [], []
        for row in range(ROWS):
            cells = act[row * COLS : (row + 1) * COLS]
            left.append(jnp.where(col == 0, 0.0, pltpu.roll(cells, 1, 0)))
            right.append(jnp.where(col == COLS - 1, 0.0, pltpu.roll(cells, COLS - 1, 0)))
        taps_ref[frame, :COLS] = jnp.zeros((COLS, WIDE), BF16)
        taps_ref[frame, COLS + PX :] = jnp.zeros((COLS, WIDE), BF16)
        inside = slice(COLS, COLS + PX)
        taps_ref[frame, inside, :LOCAL] = jnp.concatenate(left, axis=0).astype(BF16)
        taps_ref[frame, inside, LOCAL : 2 * LOCAL] = act.astype(BF16)
        taps_ref[frame, inside, 2 * LOCAL :] = jnp.concatenate(right, axis=0).astype(BF16)

    return frame_taps


def spatial_sums(taps_ref, weight_ref, frame):
    total = None
    for row_tap in range(TAPS):
        cells = slice(row_tap * COLS, row_tap * COLS + PX)
        term = jnp.dot(taps_ref[frame, cells], weight_ref[row_tap], preferred_element_type=F32)
        total = term if total is None else total + term
    return total


def spatial_send_kernel(
    lat_hbm, weight_hbm, send_ref, taps_ref, own_weight_ref, lat_ref, weight_ref, lat_sem, sems, own_sems
):
    lat_copy = pltpu.make_async_copy(lat_hbm, lat_ref, lat_sem)
    lat_copy.start()
    copies = start_copies([(first_columns(False), 0, FIRST)], weight_hbm, weight_ref, sems)
    own_copies = start_copies([(first_columns(True), 0, FIRST)], weight_hbm, own_weight_ref, own_sems)
    lat_copy.wait()
    frame_taps = spatial_taps(lat_ref, taps_ref)
    frame_taps(0)
    for copy in copies:
        copy.wait()
    frame_taps(1)
    for frame in range(2):
        send_ref[frame * PX : (frame + 1) * PX] = spatial_sums(taps_ref, weight_ref, frame).astype(BF16)
    for copy in own_copies:
        copy.wait()


def spatial_own_kernel(taps_ref, weight_ref, own_ref):
    for frame in range(2):
        own_ref[frame * PX : (frame + 1) * PX] = spatial_sums(taps_ref, weight_ref, frame).astype(BF16)


def spatial_rest_kernel(lat_hbm, weight_hbm, after_ref, *refs):
    *outs, lat_ref, weight_ref, taps_ref, total_ref, lat_sem, sems = refs
    lat_copy = pltpu.make_async_copy(lat_hbm, lat_ref, lat_sem)
    lat_copy.start()
    copies = copy_columns(False, weight_hbm, weight_ref, sems)
    lat_copy.wait()
    frame_taps = spatial_taps(lat_ref, taps_ref)
    frame_taps(0)
    for copy in copies:
        copy.wait()
    frame_taps(1)
    for frame in range(2):
        store_sums(False, frame, spatial_sums(taps_ref, weight_ref, frame), outs, total_ref)


def spatial_cost(columns):
    return pl.CostEstimate(
        flops=4 * PX * TAPS * WIDE * columns,
        bytes_accessed=2 * TAPS * WIDE * columns,
        transcendentals=2 * PX * LOCAL,
    )


def spatial_first(lat, weight):
    vmem, anywhere = pl.BlockSpec(memory_space=pltpu.VMEM), pl.BlockSpec(memory_space=pl.ANY)
    sums = jax.ShapeDtypeStruct((2 * PX, FIRST), BF16)
    columns = jax.ShapeDtypeStruct((TAPS, WIDE, FIRST), BF16)
    send, taps, own_weight = pl.pallas_call(
        spatial_send_kernel,
        in_specs=[anywhere] * 2,
        out_specs=[vmem] * 3,
        out_shape=[sums, jax.ShapeDtypeStruct((2, PX + 2 * COLS, WIDE), BF16), columns],
        scratch_shapes=[
            pltpu.VMEM((2 * PX, LOCAL), BF16),
            pltpu.VMEM(columns.shape, BF16),
            pltpu.SemaphoreType.DMA,
            pltpu.SemaphoreType.DMA((TAPS, 1)),
            pltpu.SemaphoreType.DMA((TAPS, 1)),
        ],
        compiler_params=params(),
        cost_estimate=spatial_cost(FIRST),
        name="spatial_send",
    )(lat, weight)
    own = pl.pallas_call(
        spatial_own_kernel,
        in_specs=[vmem] * 2,
        out_specs=vmem,
        out_shape=sums,
        compiler_params=params(),
        cost_estimate=spatial_cost(FIRST),
        name="spatial_own",
    )(taps, own_weight)
    return send, own


def spatial_second(lat, weight, after):
    vmem, anywhere = pl.BlockSpec(memory_space=pltpu.VMEM), pl.BlockSpec(memory_space=pl.ANY)
    columns = part_columns(False)
    return pl.pallas_call(
        spatial_rest_kernel,
        in_specs=[anywhere] * 3,
        out_specs=[vmem] * 4,
        out_shape=part_shapes(False),
        scratch_shapes=[
            pltpu.VMEM((2 * PX, LOCAL), BF16),
            pltpu.VMEM((TAPS, WIDE, columns), BF16),
            pltpu.VMEM((2, PX + 2 * COLS, WIDE), BF16),
            pltpu.VMEM((2, PX, columns), BF16),
            pltpu.SemaphoreType.DMA,
            pltpu.SemaphoreType.DMA((TAPS, 2)),
        ],
        compiler_params=params(),
        cost_estimate=spatial_cost(columns),
        name="spatial_rest",
    )(lat, weight, after)


def temporal_kernel(other, hidden_ref, across_ref, pair_ref, stats_ref, weight_hbm, after_ref, *refs):
    *outs, weight_ref, taps_ref, total_ref, sems = refs
    copies = copy_columns(other, weight_hbm, weight_ref, sems)
    seq, size = lax.axis_index("seq"), lax.axis_size("seq")
    sums = jnp.sum(stats_ref[...], axis=0, keepdims=True) * (1.0 / (GROUP * 2 * PX * size))
    squares = pltpu.roll(jnp.broadcast_to(sums, (8, 128)), 128 - LOCAL_GROUPS, 1)[0:1]
    both = exact_dot(jnp.concatenate([sums, squares, jnp.zeros((6, 128), F32)], axis=0), lane_to_group())
    mean = both[0:1]
    var = both[1:2] - mean * mean
    scale = lax.rsqrt(var + EPS)

    def act(values):
        return silu((values - mean) * scale)

    def put(values, *places):
        values = values.astype(BF16)
        for frame, tap in places:
            taps_ref[frame, :, tap * LOCAL : (tap + 1) * LOCAL] = values

    def halo(even_ref, odd_ref, edge):
        values = jnp.where(seq % 2 == 0, unpack(even_ref), unpack(odd_ref))
        return act(values.astype(F32)) * jnp.where(edge, 0.0, 1.0)

    put(halo(across_ref, pair_ref, seq == 0), (0, 0))
    put(act(hidden_ref[:PX]), (0, 1), (1, 0))
    put(act(hidden_ref[PX:]), (0, 2), (1, 1))
    for copy in copies:
        copy.wait()
    put(halo(pair_ref, across_ref, seq == size - 1), (1, 2))
    for frame in range(2):
        total = jnp.dot(taps_ref[frame], weight_ref[0], preferred_element_type=F32)
        store_sums(other, frame, total, outs, total_ref)


def temporal_call(hidden, halos, stats, weight, after, other):
    vmem = pl.BlockSpec(memory_space=pltpu.VMEM)
    shapes, columns = part_shapes(other), part_columns(other)
    return pl.pallas_call(
        functools.partial(temporal_kernel, other),
        in_specs=[vmem] * 4 + [pl.BlockSpec(memory_space=pl.ANY)] * 2,
        out_specs=[vmem] * len(shapes),
        out_shape=shapes,
        scratch_shapes=[
            pltpu.VMEM((1, WIDE, columns), BF16),
            pltpu.VMEM((2, PX, WIDE), BF16),
            pltpu.VMEM((2, PX, columns), BF16),
            pltpu.SemaphoreType.DMA((1, 2)),
        ],
        compiler_params=params(),
        cost_estimate=pl.CostEstimate(
            flops=4 * PX * WIDE * columns,
            bytes_accessed=2 * WIDE * columns,
            transcendentals=4 * PX * LOCAL,
        ),
        name="temporal",
    )(hidden, *halos[::-1], stats, weight, after)


def chip_sum_kernel(own_ref, got_ref, out_ref):
    out_ref[...] = (own_ref[...].astype(F32) + got_ref[...].astype(F32)).astype(BF16)


def chip_sum(own, got):
    return pl.pallas_call(
        chip_sum_kernel,
        out_shape=jax.ShapeDtypeStruct(own.shape, BF16),
        compiler_params=pltpu.CompilerParams(vmem_limit_bytes=8 * 1024 * 1024),
        cost_estimate=pl.CostEstimate(flops=4 * 10**9, bytes_accessed=6 * own.size, transcendentals=0),
        name="chip_sum",
    )(own, got)


def chip_part(own_ref, core_refs, frame):
    cols = slice(frame * LOCAL, (frame + 1) * LOCAL)
    core = jnp.concatenate([ref[:, cols] for ref in core_refs], axis=0)
    return own_ref[:, cols].astype(F32) + core.astype(F32)


def half_part(first_ref, rest_ref, frame):
    first = first_ref[frame * PX : (frame + 1) * PX].astype(F32)
    rest = rest_ref[:, frame * REST : (frame + 1) * REST].astype(F32)
    return jnp.where(
        lax.axis_index("ch") % 2 == 0,
        jnp.concatenate([first, rest], axis=1),
        jnp.concatenate([rest, first], axis=1),
    )


def small_cost():
    return pl.CostEstimate(flops=10 * PX * LOCAL, bytes_accessed=20 * PX * LOCAL, transcendentals=0)


def base_kernel(lat_ref, own_ref, *refs):
    *cores, base_ref = refs
    for frame in range(2):
        cells = slice(frame * PX, (frame + 1) * PX)
        base_ref[cells] = lat_ref[cells].astype(F32) + chip_part(own_ref, cores, frame)


def base_call(lat, own, cores):
    return pl.pallas_call(
        base_kernel,
        out_shape=jax.ShapeDtypeStruct((2 * PX, LOCAL), F32),
        compiler_params=params(),
        cost_estimate=small_cost(),
        name="base",
    )(lat, own, *cores)


def hidden_kernel(base_ref, half_first, half_rest, hidden_ref, edges_ref, stats_ref):
    odd = lax.axis_index("seq") % 2
    sums, squares = 0.0, 0.0
    for frame in range(2):
        cells = slice(frame * PX, (frame + 1) * PX)
        hidden = base_ref[cells] + half_part(half_first, half_rest, frame)
        hidden_ref[cells] = hidden
        slot = 1 - odd if frame == 0 else odd
        edges_ref[pl.ds(pl.multiple_of(slot * (PX // 2), PX // 2), PX // 2)] = pack(hidden).astype(BF16)
        sums += jnp.sum(hidden, axis=0, keepdims=True)
        squares += jnp.sum(hidden * hidden, axis=0, keepdims=True)
    both = jnp.concatenate([sums, squares, jnp.zeros((6, LOCAL), F32)], axis=0)
    both = exact_dot(both, group_to_lane())
    row = both[0:1] + pltpu.roll(both, LOCAL_GROUPS, 1)[1:2]
    stats_ref[...] = jnp.broadcast_to(row, stats_ref.shape)


def hidden_call(base, half_first, half_rest, size):
    return pl.pallas_call(
        hidden_kernel,
        out_shape=[
            jax.ShapeDtypeStruct((2 * PX, LOCAL), F32),
            jax.ShapeDtypeStruct((PX, 2 * LOCAL), BF16),
            jax.ShapeDtypeStruct((size, 128), F32),
        ],
        compiler_params=params(),
        cost_estimate=small_cost(),
        name="hidden",
    )(base, half_first, half_rest)


def branch_weight(mix_ref):
    return 1.0 - jax.nn.sigmoid(jnp.full((1, LOCAL), mix_ref[0], F32))


def mixed_kernel(mix_ref, hidden_ref, own_ref, *refs):
    *cores, mixed_ref = refs
    for frame in range(2):
        cells = slice(frame * PX, (frame + 1) * PX)
        mixed_ref[cells] = hidden_ref[cells] + branch_weight(mix_ref) * chip_part(own_ref, cores, frame)


def blend_kernel(mix_ref, mixed_ref, half_first, half_rest, out_hbm, out_ref, sems):
    copies = []
    for frame in range(2):
        cells = slice(frame * PX, (frame + 1) * PX)
        half = half_part(half_first, half_rest, frame)
        out_ref[cells] = (mixed_ref[cells] + branch_weight(mix_ref) * half).astype(BF16)
        copies.append(pltpu.make_async_copy(out_ref.at[cells], out_hbm.at[cells], sems.at[frame]))
        copies[-1].start()
    for copy in copies:
        copy.wait()


def blend_call(mix, *arrays):
    whole = pl.BlockSpec(memory_space=pltpu.VMEM)
    return pl.pallas_call(
        blend_kernel,
        in_specs=[pl.BlockSpec(memory_space=pltpu.SMEM)] + [whole] * len(arrays),
        out_specs=pl.BlockSpec(memory_space=pl.ANY),
        out_shape=jax.ShapeDtypeStruct((2 * PX, LOCAL), BF16),
        scratch_shapes=[pltpu.VMEM((2 * PX, LOCAL), BF16), pltpu.SemaphoreType.DMA((2,))],
        compiler_params=params(),
        cost_estimate=small_cost(),
        name="blend",
    )(mix, *arrays)


def mix_call(kernel, mix, dtype, name, *arrays):
    whole = pl.BlockSpec(memory_space=pltpu.VMEM)
    return pl.pallas_call(
        kernel,
        in_specs=[pl.BlockSpec(memory_space=pltpu.SMEM)] + [whole] * len(arrays),
        out_specs=whole,
        out_shape=jax.ShapeDtypeStruct((2 * PX, LOCAL), dtype),
        compiler_params=params(),
        cost_estimate=small_cost(),
        name=name,
    )(mix, *arrays)


def to_core(array, pieces=1):
    rows = array.shape[0] // pieces
    return [lax.ppermute(array[i * rows : (i + 1) * rows], "ch", CORE_SWAP) for i in range(pieces)]


def to_half(array):
    return lax.ppermute(array, "ch", HALF_SWAP)


def settle(array, after):
    anywhere = pl.BlockSpec(memory_space=pl.ANY)
    return pl.pallas_call(
        lambda in_ref, after_ref, out_ref: None,
        in_specs=[anywhere, anywhere],
        out_specs=anywhere,
        out_shape=jax.ShapeDtypeStruct(array.shape, array.dtype),
        input_output_aliases={0: 0},
        compiler_params=pltpu.CompilerParams(vmem_limit_bytes=1024 * 1024),
        cost_estimate=pl.CostEstimate(flops=10**10, bytes_accessed=0, transcendentals=0),
        name="settle",
    )(array, after)


def reduce_channels(first, second, combine):
    send, own = first()
    chip = chip_sum(own, *to_core(send))
    half_first = to_half(chip)
    send_rest, own_rest, send, own = second(chip)
    half_rest = to_half(chip_sum(own_rest, *to_core(send_rest)))
    combined = combine(own, to_core(send, CORE_PIECES))
    return combined, settle(half_first, combined), half_rest


def per_device(latents, spatial_weight, temporal_weight, mix_factor):
    size = lax.axis_size("seq")
    lat = latents.transpose(0, 2, 3, 1).reshape(2 * PX, LOCAL)
    lat_hbm = pltpu.with_memory_space_constraint(lat, pltpu.HBM)
    weight_s = pltpu.with_memory_space_constraint(spatial_weight.reshape(TAPS, WIDE, CH), pltpu.HBM)
    weight_t = temporal_weight.reshape(1, WIDE, CH)
    base, half_first, half_rest = reduce_channels(
        lambda: spatial_first(lat_hbm, weight_s),
        lambda after: spatial_second(lat_hbm, weight_s, after),
        lambda own, cores: base_call(lat, own, cores),
    )
    hidden, edges, stats = hidden_call(base, half_first, half_rest, size)
    halos = []
    for start in range(2):
        pairs = [(i, i + 1) for i in range(start, size - 1, 2)]
        edge = edges[start * (PX // 2) : (start + 1) * (PX // 2)]
        halos.append(lax.ppermute(edge, "seq", pairs + [(b, a) for a, b in pairs]))
    stats = lax.all_to_all(stats, "seq", 0, 0, tiled=True)
    mixed, half_first, half_rest = reduce_channels(
        lambda: temporal_call(hidden, halos, stats, weight_t, hidden, True),
        lambda after: temporal_call(hidden, halos, stats, weight_t, after, False),
        lambda own, cores: mix_call(mixed_kernel, mix_factor, F32, "mixed", hidden, own, *cores),
    )
    out = blend_call(mix_factor, mixed, half_first, half_rest)
    return out.reshape(2, ROWS, COLS, LOCAL).transpose(0, 3, 1, 2)


def solution(mesh):
    placed = (P("seq", "ch", None, None), P(None, None, "ch", None), P(None, "ch", None), P())
    return jax.shard_map(
        per_device,
        mesh=mesh,
        in_specs=placed,
        out_specs=P("seq", "ch", None, None),
        check_vma=False,
    )
```

```python
import functools

import jax
import jax.numpy as jnp
from jax import lax
from jax.experimental import pallas as pl
from jax.experimental.pallas import tpu as pltpu
from jax.sharding import PartitionSpec as P

CH = 1280
GROUPS = 32
GROUP = CH // GROUPS
ROWS = 16
COLS = 32
PX = ROWS * COLS
LOCAL = CH // 4
LOCAL_GROUPS = LOCAL // GROUP
TAPS = 3
WIDE = TAPS * LOCAL
HALF = CH // 2
EPS = 1e-05

CORE_SWAP = [(0, 1), (1, 0), (2, 3), (3, 2)]
HALF_SWAP = [(0, 2), (2, 0), (1, 3), (3, 1)]
FIRST = 256
REST = LOCAL - FIRST
CORE_PIECES = 2
VMEM_LIMIT = 40 * 1024 * 1024
BF16 = jnp.bfloat16
F32 = jnp.float32
HIGHEST = lax.Precision.HIGHEST


def params():
    return pltpu.CompilerParams(vmem_limit_bytes=VMEM_LIMIT)


def silu(v):
    half = 0.5 * v
    return half + half * jnp.tanh(half)


def group_of(channel):
    return (channel * 205) >> 13


def group_block():
    row = lax.broadcasted_iota(jnp.int32, (LOCAL, LOCAL), 0)
    col = lax.broadcasted_iota(jnp.int32, (LOCAL, LOCAL), 1)
    return jnp.where(group_of(row) == group_of(col), 1.0, 0.0)


def group_to_lane():
    row = lax.broadcasted_iota(jnp.int32, (LOCAL, 128), 0)
    lane = lax.broadcasted_iota(jnp.int32, (LOCAL, 128), 1)
    return jnp.where(group_of(row) == lane, 1.0, 0.0)


def lane_to_group():
    lane = lax.broadcasted_iota(jnp.int32, (128, LOCAL), 0)
    col = lax.broadcasted_iota(jnp.int32, (128, LOCAL), 1)
    return jnp.where(group_of(col) == lane, 1.0, 0.0)


def exact_dot(a, b):
    return jnp.dot(a, b, precision=HIGHEST, preferred_element_type=F32)


def pack(block):
    return jnp.concatenate([block[: PX // 2], block[PX // 2 :]], axis=1)


def unpack(ref):
    return jnp.concatenate([ref[:, :LOCAL], ref[:, LOCAL:]], axis=0)


def start_copies(pieces, weight_hbm, weight_ref, sems):
    copies = []
    for tap in range(weight_hbm.shape[0]):
        for i, (start, to, width) in enumerate(pieces):
            source = weight_hbm.at[tap, :, pl.ds(pl.multiple_of(start, 128), width)]
            copy = pltpu.make_async_copy(source, weight_ref.at[tap, :, to : to + width], sems.at[tap, i])
            copy.start()
            copies.append(copy)
    return copies


def first_columns(own):
    index = lax.axis_index("ch")
    half, core = index // 2, index % 2
    core = core if own else 1 - core
    return (1 - half) * HALF + core * (HALF - FIRST)


def copy_columns(other, weight_hbm, weight_ref, sems):
    if other:
        pieces = [(first_columns(True), 0, FIRST), (first_columns(False), FIRST, FIRST)]
    else:
        half = lax.axis_index("ch") // 2
        pieces = [((1 - half) * HALF + FIRST, 0, 2 * REST), (half * HALF, 2 * REST, HALF)]
    return start_copies(pieces, weight_hbm, weight_ref, sems)


def store_sums(other, frame, total, outs, total_ref):
    if other:
        send_ref, own_ref = outs
        cells = slice(frame * PX, (frame + 1) * PX)
        own_ref[cells] = total[:, :FIRST].astype(BF16)
        send_ref[cells] = total[:, FIRST:].astype(BF16)
    else:
        total_ref[frame] = total.astype(BF16)
        if frame == 1:
            split_second(total_ref, *outs)


def split_second(total_ref, send_rest, own_rest, send_ref, own_ref):
    core = lax.axis_index("ch") % 2

    def copy(ref, first, width):
        for frame in range(2):
            ref[:, frame * width : (frame + 1) * width] = total_ref[frame, :, first : first + width]

    @pl.when(core == 0)
    def _():
        copy(own_rest, 0, REST)
        copy(send_rest, REST, REST)
        copy(own_ref, 2 * REST, LOCAL)
        copy(send_ref, 2 * REST + LOCAL, LOCAL)

    @pl.when(core == 1)
    def _():
        copy(own_rest, REST, REST)
        copy(send_rest, 0, REST)
        copy(own_ref, 2 * REST + LOCAL, LOCAL)
        copy(send_ref, 2 * REST, LOCAL)


def part_shapes(other):
    if other:
        return [jax.ShapeDtypeStruct((2 * PX, FIRST), BF16)] * 2
    rest, own = jax.ShapeDtypeStruct((PX, 2 * REST), BF16), jax.ShapeDtypeStruct((PX, 2 * LOCAL), BF16)
    return [rest, rest, own, own]


def part_columns(other):
    return 2 * FIRST if other else 2 * REST + HALF


def spatial_taps(lat_ref, taps_ref):
    rows = []
    for frame in range(2):
        lat = lat_ref[frame * PX : (frame + 1) * PX].astype(F32)
        rows.append(jnp.sum(lat, axis=0, keepdims=True))
        rows.append(jnp.sum(lat * lat, axis=0, keepdims=True))
    means = jnp.concatenate(rows + [jnp.zeros((4, LOCAL), F32)], axis=0)
    means = exact_dot(means, group_block()) * (1.0 / (GROUP * PX))
    col = lax.broadcasted_iota(jnp.int32, (COLS, LOCAL), 0)
    def frame_taps(frame):
        mean = means[2 * frame : 2 * frame + 1]
        var = means[2 * frame + 1 : 2 * frame + 2] - mean * mean
        lat = lat_ref[frame * PX : (frame + 1) * PX].astype(F32)
        act = silu((lat - mean) * lax.rsqrt(var + EPS))
        left, right = [], []
        for row in range(ROWS):
            cells = act[row * COLS : (row + 1) * COLS]
            left.append(jnp.where(col == 0, 0.0, pltpu.roll(cells, 1, 0)))
            right.append(jnp.where(col == COLS - 1, 0.0, pltpu.roll(cells, COLS - 1, 0)))
        taps_ref[frame, :COLS] = jnp.zeros((COLS, WIDE), BF16)
        taps_ref[frame, COLS + PX :] = jnp.zeros((COLS, WIDE), BF16)
        inside = slice(COLS, COLS + PX)
        taps_ref[frame, inside, :LOCAL] = jnp.concatenate(left, axis=0).astype(BF16)
        taps_ref[frame, inside, LOCAL : 2 * LOCAL] = act.astype(BF16)
        taps_ref[frame, inside, 2 * LOCAL :] = jnp.concatenate(right, axis=0).astype(BF16)

    return frame_taps


def spatial_sums(taps_ref, weight_ref, frame):
    total = None
    for row_tap in range(TAPS):
        cells = slice(row_tap * COLS, row_tap * COLS + PX)
        term = jnp.dot(taps_ref[frame, cells], weight_ref[row_tap], preferred_element_type=F32)
        total = term if total is None else total + term
    return total


def spatial_send_kernel(
    lat_hbm, weight_hbm, send_ref, taps_ref, own_weight_ref, lat_ref, weight_ref, lat_sem, sems, own_sems
):
    lat_copy = pltpu.make_async_copy(lat_hbm, lat_ref, lat_sem)
    lat_copy.start()
    copies = start_copies([(first_columns(False), 0, FIRST)], weight_hbm, weight_ref, sems)
    own_copies = start_copies([(first_columns(True), 0, FIRST)], weight_hbm, own_weight_ref, own_sems)
    lat_copy.wait()
    frame_taps = spatial_taps(lat_ref, taps_ref)
    frame_taps(0)
    for copy in copies:
        copy.wait()
    frame_taps(1)
    for frame in range(2):
        send_ref[frame * PX : (frame + 1) * PX] = spatial_sums(taps_ref, weight_ref, frame).astype(BF16)
    for copy in own_copies:
        copy.wait()


def spatial_own_kernel(taps_ref, weight_ref, own_ref):
    for frame in range(2):
        own_ref[frame * PX : (frame + 1) * PX] = spatial_sums(taps_ref, weight_ref, frame).astype(BF16)


def spatial_rest_kernel(lat_hbm, weight_hbm, after_ref, *refs):
    *outs, lat_ref, weight_ref, taps_ref, total_ref, lat_sem, sems = refs
    lat_copy = pltpu.make_async_copy(lat_hbm, lat_ref, lat_sem)
    lat_copy.start()
    copies = copy_columns(False, weight_hbm, weight_ref, sems)
    lat_copy.wait()
    frame_taps = spatial_taps(lat_ref, taps_ref)
    frame_taps(0)
    for copy in copies:
        copy.wait()
    frame_taps(1)
    for frame in range(2):
        store_sums(False, frame, spatial_sums(taps_ref, weight_ref, frame), outs, total_ref)


def spatial_cost(columns):
    return pl.CostEstimate(
        flops=4 * PX * TAPS * WIDE * columns,
        bytes_accessed=2 * TAPS * WIDE * columns,
        transcendentals=2 * PX * LOCAL,
    )


def spatial_first(lat, weight):
    vmem, anywhere = pl.BlockSpec(memory_space=pltpu.VMEM), pl.BlockSpec(memory_space=pl.ANY)
    sums = jax.ShapeDtypeStruct((2 * PX, FIRST), BF16)
    columns = jax.ShapeDtypeStruct((TAPS, WIDE, FIRST), BF16)
    send, taps, own_weight = pl.pallas_call(
        spatial_send_kernel,
        in_specs=[anywhere] * 2,
        out_specs=[vmem] * 3,
        out_shape=[sums, jax.ShapeDtypeStruct((2, PX + 2 * COLS, WIDE), BF16), columns],
        scratch_shapes=[
            pltpu.VMEM((2 * PX, LOCAL), BF16),
            pltpu.VMEM(columns.shape, BF16),
            pltpu.SemaphoreType.DMA,
            pltpu.SemaphoreType.DMA((TAPS, 1)),
            pltpu.SemaphoreType.DMA((TAPS, 1)),
        ],
        compiler_params=params(),
        cost_estimate=spatial_cost(FIRST),
        name="spatial_send",
    )(lat, weight)
    own = pl.pallas_call(
        spatial_own_kernel,
        in_specs=[vmem] * 2,
        out_specs=vmem,
        out_shape=sums,
        compiler_params=params(),
        cost_estimate=spatial_cost(FIRST),
        name="spatial_own",
    )(taps, own_weight)
    return send, own


def spatial_second(lat, weight, after):
    vmem, anywhere = pl.BlockSpec(memory_space=pltpu.VMEM), pl.BlockSpec(memory_space=pl.ANY)
    columns = part_columns(False)
    return pl.pallas_call(
        spatial_rest_kernel,
        in_specs=[anywhere] * 3,
        out_specs=[vmem] * 4,
        out_shape=part_shapes(False),
        scratch_shapes=[
            pltpu.VMEM((2 * PX, LOCAL), BF16),
            pltpu.VMEM((TAPS, WIDE, columns), BF16),
            pltpu.VMEM((2, PX + 2 * COLS, WIDE), BF16),
            pltpu.VMEM((2, PX, columns), BF16),
            pltpu.SemaphoreType.DMA,
            pltpu.SemaphoreType.DMA((TAPS, 2)),
        ],
        compiler_params=params(),
        cost_estimate=spatial_cost(columns),
        name="spatial_rest",
    )(lat, weight, after)


def temporal_taps(hidden_ref, pair_ref, across_ref, stats_ref, taps_ref, copies):
    seq, size = lax.axis_index("seq"), lax.axis_size("seq")
    sums = jnp.sum(stats_ref[...], axis=0, keepdims=True) * (1.0 / (GROUP * 2 * PX * size))
    squares = pltpu.roll(jnp.broadcast_to(sums, (8, 128)), 128 - LOCAL_GROUPS, 1)[0:1]
    both = exact_dot(jnp.concatenate([sums, squares, jnp.zeros((6, 128), F32)], axis=0), lane_to_group())
    mean = both[0:1]
    var = both[1:2] - mean * mean
    scale = lax.rsqrt(var + EPS)

    def act(values):
        return silu((values - mean) * scale)

    def put(values, *places):
        values = values.astype(BF16)
        for frame, tap in places:
            taps_ref[frame, :, tap * LOCAL : (tap + 1) * LOCAL] = values

    def halo(even_ref, odd_ref, edge):
        values = jnp.where(seq % 2 == 0, unpack(even_ref), unpack(odd_ref))
        return act(values.astype(F32)) * jnp.where(edge, 0.0, 1.0)

    put(halo(across_ref, pair_ref, seq == 0), (0, 0))
    put(act(hidden_ref[:PX]), (0, 1), (1, 0))
    put(act(hidden_ref[PX:]), (0, 2), (1, 1))
    for copy in copies:
        copy.wait()
    put(halo(pair_ref, across_ref, seq == size - 1), (1, 2))


def temporal_sums(taps_ref, weight_ref, frame):
    return jnp.dot(taps_ref[frame], weight_ref[0], preferred_element_type=F32)


def temporal_send_kernel(*refs):
    *inputs, weight_hbm, send_ref, taps_ref, own_weight_ref, weight_ref, sems, own_sems = refs
    copies = start_copies([(first_columns(False), 0, FIRST)], weight_hbm, weight_ref, sems)
    own_copies = start_copies([(first_columns(True), 0, FIRST)], weight_hbm, own_weight_ref, own_sems)
    temporal_taps(*inputs, taps_ref, copies)
    for frame in range(2):
        send_ref[frame * PX : (frame + 1) * PX] = temporal_sums(taps_ref, weight_ref, frame).astype(BF16)
    for copy in own_copies:
        copy.wait()


def temporal_own_kernel(taps_ref, weight_ref, own_ref):
    for frame in range(2):
        own_ref[frame * PX : (frame + 1) * PX] = temporal_sums(taps_ref, weight_ref, frame).astype(BF16)


def temporal_rest_kernel(*refs):
    *inputs, weight_hbm, after_ref = refs[:6]
    *outs, weight_ref, taps_ref, total_ref, sems = refs[6:]
    copies = copy_columns(False, weight_hbm, weight_ref, sems)
    temporal_taps(*inputs, taps_ref, copies)
    for frame in range(2):
        store_sums(False, frame, temporal_sums(taps_ref, weight_ref, frame), outs, total_ref)


def temporal_cost(columns):
    return pl.CostEstimate(
        flops=4 * PX * WIDE * columns,
        bytes_accessed=2 * WIDE * columns,
        transcendentals=4 * PX * LOCAL,
    )


def temporal_first(hidden, halos, stats, weight):
    vmem, anywhere = pl.BlockSpec(memory_space=pltpu.VMEM), pl.BlockSpec(memory_space=pl.ANY)
    sums = jax.ShapeDtypeStruct((2 * PX, FIRST), BF16)
    columns = jax.ShapeDtypeStruct((1, WIDE, FIRST), BF16)
    send, taps, own_weight = pl.pallas_call(
        temporal_send_kernel,
        in_specs=[vmem] * 4 + [anywhere],
        out_specs=[vmem] * 3,
        out_shape=[sums, jax.ShapeDtypeStruct((2, PX, WIDE), BF16), columns],
        scratch_shapes=[
            pltpu.VMEM(columns.shape, BF16),
            pltpu.SemaphoreType.DMA((1, 1)),
            pltpu.SemaphoreType.DMA((1, 1)),
        ],
        compiler_params=params(),
        cost_estimate=temporal_cost(FIRST),
        name="temporal_send",
    )(hidden, *halos, stats, weight)
    own = pl.pallas_call(
        temporal_own_kernel,
        in_specs=[vmem] * 2,
        out_specs=vmem,
        out_shape=sums,
        compiler_params=params(),
        cost_estimate=temporal_cost(FIRST),
        name="temporal_own",
    )(taps, own_weight)
    return send, own


def temporal_second(hidden, halos, stats, weight, after):
    vmem, anywhere = pl.BlockSpec(memory_space=pltpu.VMEM), pl.BlockSpec(memory_space=pl.ANY)
    columns = part_columns(False)
    return pl.pallas_call(
        temporal_rest_kernel,
        in_specs=[vmem] * 4 + [anywhere] * 2,
        out_specs=[vmem] * 4,
        out_shape=part_shapes(False),
        scratch_shapes=[
            pltpu.VMEM((1, WIDE, columns), BF16),
            pltpu.VMEM((2, PX, WIDE), BF16),
            pltpu.VMEM((2, PX, columns), BF16),
            pltpu.SemaphoreType.DMA((1, 2)),
        ],
        compiler_params=params(),
        cost_estimate=temporal_cost(columns),
        name="temporal_rest",
    )(hidden, *halos, stats, weight, after)


def chip_sum_kernel(own_ref, got_ref, out_ref):
    out_ref[...] = (own_ref[...].astype(F32) + got_ref[...].astype(F32)).astype(BF16)


def chip_sum(own, got):
    return pl.pallas_call(
        chip_sum_kernel,
        out_shape=jax.ShapeDtypeStruct(own.shape, BF16),
        compiler_params=pltpu.CompilerParams(vmem_limit_bytes=8 * 1024 * 1024),
        cost_estimate=pl.CostEstimate(flops=4 * 10**9, bytes_accessed=6 * own.size, transcendentals=0),
        name="chip_sum",
    )(own, got)


def chip_part(own_ref, core_refs, frame):
    cols = slice(frame * LOCAL, (frame + 1) * LOCAL)
    core = jnp.concatenate([ref[:, cols] for ref in core_refs], axis=0)
    return own_ref[:, cols].astype(F32) + core.astype(F32)


def half_part(first_ref, rest_ref, frame):
    first = first_ref[frame * PX : (frame + 1) * PX].astype(F32)
    rest = rest_ref[:, frame * REST : (frame + 1) * REST].astype(F32)
    return jnp.where(
        lax.axis_index("ch") % 2 == 0,
        jnp.concatenate([first, rest], axis=1),
        jnp.concatenate([rest, first], axis=1),
    )


def small_cost():
    return pl.CostEstimate(flops=10 * PX * LOCAL, bytes_accessed=20 * PX * LOCAL, transcendentals=0)


def base_kernel(lat_ref, own_ref, *refs):
    *cores, base_ref = refs
    for frame in range(2):
        cells = slice(frame * PX, (frame + 1) * PX)
        base_ref[cells] = lat_ref[cells].astype(F32) + chip_part(own_ref, cores, frame)


def base_call(lat, own, cores):
    return pl.pallas_call(
        base_kernel,
        out_shape=jax.ShapeDtypeStruct((2 * PX, LOCAL), F32),
        compiler_params=params(),
        cost_estimate=small_cost(),
        name="base",
    )(lat, own, *cores)


def hidden_kernel(base_ref, half_first, half_rest, hidden_ref, edges_ref, stats_ref):
    odd = lax.axis_index("seq") % 2
    sums, squares = 0.0, 0.0
    for frame in range(2):
        cells = slice(frame * PX, (frame + 1) * PX)
        hidden = base_ref[cells] + half_part(half_first, half_rest, frame)
        hidden_ref[cells] = hidden
        slot = 1 - odd if frame == 0 else odd
        edges_ref[pl.ds(pl.multiple_of(slot * (PX // 2), PX // 2), PX // 2)] = pack(hidden).astype(BF16)
        sums += jnp.sum(hidden, axis=0, keepdims=True)
        squares += jnp.sum(hidden * hidden, axis=0, keepdims=True)
    both = jnp.concatenate([sums, squares, jnp.zeros((6, LOCAL), F32)], axis=0)
    both = exact_dot(both, group_to_lane())
    row = both[0:1] + pltpu.roll(both, LOCAL_GROUPS, 1)[1:2]
    stats_ref[...] = jnp.broadcast_to(row, stats_ref.shape)


def hidden_call(base, half_first, half_rest, size):
    return pl.pallas_call(
        hidden_kernel,
        out_shape=[
            jax.ShapeDtypeStruct((2 * PX, LOCAL), F32),
            jax.ShapeDtypeStruct((PX, 2 * LOCAL), BF16),
            jax.ShapeDtypeStruct((size, 128), F32),
        ],
        compiler_params=params(),
        cost_estimate=small_cost(),
        name="hidden",
    )(base, half_first, half_rest)


def branch_weight(mix_ref):
    return 1.0 - jax.nn.sigmoid(jnp.full((1, LOCAL), mix_ref[0], F32))


def mixed_kernel(mix_ref, hidden_ref, own_ref, *refs):
    *cores, mixed_ref = refs
    for frame in range(2):
        cells = slice(frame * PX, (frame + 1) * PX)
        mixed_ref[cells] = hidden_ref[cells] + branch_weight(mix_ref) * chip_part(own_ref, cores, frame)


def blend_kernel(mix_ref, mixed_ref, half_first, half_rest, out_hbm, out_ref, sems):
    copies = []
    for frame in range(2):
        cells = slice(frame * PX, (frame + 1) * PX)
        half = half_part(half_first, half_rest, frame)
        out_ref[cells] = (mixed_ref[cells] + branch_weight(mix_ref) * half).astype(BF16)
        copies.append(pltpu.make_async_copy(out_ref.at[cells], out_hbm.at[cells], sems.at[frame]))
        copies[-1].start()
    for copy in copies:
        copy.wait()


def blend_call(mix, *arrays):
    whole = pl.BlockSpec(memory_space=pltpu.VMEM)
    return pl.pallas_call(
        blend_kernel,
        in_specs=[pl.BlockSpec(memory_space=pltpu.SMEM)] + [whole] * len(arrays),
        out_specs=pl.BlockSpec(memory_space=pl.ANY),
        out_shape=jax.ShapeDtypeStruct((2 * PX, LOCAL), BF16),
        scratch_shapes=[pltpu.VMEM((2 * PX, LOCAL), BF16), pltpu.SemaphoreType.DMA((2,))],
        compiler_params=params(),
        cost_estimate=small_cost(),
        name="blend",
    )(mix, *arrays)


def mix_call(kernel, mix, dtype, name, *arrays):
    whole = pl.BlockSpec(memory_space=pltpu.VMEM)
    return pl.pallas_call(
        kernel,
        in_specs=[pl.BlockSpec(memory_space=pltpu.SMEM)] + [whole] * len(arrays),
        out_specs=whole,
        out_shape=jax.ShapeDtypeStruct((2 * PX, LOCAL), dtype),
        compiler_params=params(),
        cost_estimate=small_cost(),
        name=name,
    )(mix, *arrays)


def to_core(array, pieces=1):
    rows = array.shape[0] // pieces
    return [lax.ppermute(array[i * rows : (i + 1) * rows], "ch", CORE_SWAP) for i in range(pieces)]


def to_half(array):
    return lax.ppermute(array, "ch", HALF_SWAP)


def settle(array, after):
    anywhere = pl.BlockSpec(memory_space=pl.ANY)
    return pl.pallas_call(
        lambda in_ref, after_ref, out_ref: None,
        in_specs=[anywhere, anywhere],
        out_specs=anywhere,
        out_shape=jax.ShapeDtypeStruct(array.shape, array.dtype),
        input_output_aliases={0: 0},
        compiler_params=pltpu.CompilerParams(vmem_limit_bytes=1024 * 1024),
        cost_estimate=pl.CostEstimate(flops=10**10, bytes_accessed=0, transcendentals=0),
        name="settle",
    )(array, after)


def reduce_channels(first, second, combine):
    send, own = first()
    chip = chip_sum(own, *to_core(send))
    half_first = to_half(chip)
    send_rest, own_rest, send, own = second(chip)
    half_rest = to_half(chip_sum(own_rest, *to_core(send_rest)))
    combined = combine(own, to_core(send, CORE_PIECES))
    return combined, settle(half_first, combined), half_rest


def per_device(latents, spatial_weight, temporal_weight, mix_factor):
    size = lax.axis_size("seq")
    lat = latents.transpose(0, 2, 3, 1).reshape(2 * PX, LOCAL)
    lat_hbm = pltpu.with_memory_space_constraint(lat, pltpu.HBM)
    weight_s = pltpu.with_memory_space_constraint(spatial_weight.reshape(TAPS, WIDE, CH), pltpu.HBM)
    weight_t = temporal_weight.reshape(1, WIDE, CH)
    base, half_first, half_rest = reduce_channels(
        lambda: spatial_first(lat_hbm, weight_s),
        lambda after: spatial_second(lat_hbm, weight_s, after),
        lambda own, cores: base_call(lat, own, cores),
    )
    hidden, edges, stats = hidden_call(base, half_first, half_rest, size)
    halos = []
    for start in range(2):
        pairs = [(i, i + 1) for i in range(start, size - 1, 2)]
        edge = edges[start * (PX // 2) : (start + 1) * (PX // 2)]
        halos.append(lax.ppermute(edge, "seq", pairs + [(b, a) for a, b in pairs]))
    stats = lax.all_to_all(stats, "seq", 0, 0, tiled=True)
    mixed, half_first, half_rest = reduce_channels(
        lambda: temporal_first(hidden, halos, stats, weight_t),
        lambda after: temporal_second(hidden, halos, stats, weight_t, after),
        lambda own, cores: mix_call(mixed_kernel, mix_factor, F32, "mixed", hidden, own, *cores),
    )
    out = blend_call(mix_factor, mixed, half_first, half_rest)
    return out.reshape(2, ROWS, COLS, LOCAL).transpose(0, 3, 1, 2)


def solution(mesh):
    placed = (P("seq", "ch", None, None), P(None, None, "ch", None), P(None, "ch", None), P())
    return jax.shard_map(
        per_device,
        mesh=mesh,
        in_specs=placed,
        out_specs=P("seq", "ch", None, None),
        check_vma=False,
    )
```
